1024 devices in a mesh: dp: 128 (over z, y), expert: 8 (over x, core).
Axes of the slice: x: 4, y: 4, z: 32, core: 2. Of those that a mesh axis runs over, the one named last changes fastest.
Arguments:
- tokens: bfloat16 [131072, 1024], P(('dp', 'expert')), may hold values from -6 to 6
- expert_ids: int32 [131072, 2], P(('dp', 'expert')), may hold values from 0 to 7, all different within a row; in each aligned block of 128 rows (0 to 127, 128 to 255, ...) at most 48 rows name the same one
- combine: float32 [131072, 2], P(('dp', 'expert')), may hold values from 0.2 to 1
- w_gate: bfloat16 [8, 1024, 768], P('expert', 'dp'), may hold values from -0.1875 to 0.1875
- w_up: bfloat16 [8, 1024, 768], P('expert', 'dp'), may hold values from -0.1875 to 0.1875
- w_down: bfloat16 [8, 1024, 768], P('expert', 'dp'), may hold values from -0.21875 to 0.21875
- cotangent: bfloat16 [131072, 1024], P(('dp', 'expert')), may hold values from -6 to 6
Outputs:
- mixed: bfloat16 [131072, 1024], P(('dp', 'expert'))
- input_grad: bfloat16 [131072, 1024], P(('dp', 'expert'))
- combine_grad: float32 [131072, 2], P(('dp', 'expert'))
The draws below stay inside these ranges and needn't reach their ends.
Inputs may be any that keep to these rules, and one draw needn't show every extreme that they name: `expert_ids`: among the rows of one device (128 tokens) no expert is named more than 48 times, and in every draw some expert is named exactly 48 times by the rows of some device; a token names 2 different experts.
All inputs are finite; a program needn't handle non-finite values.
Results may differ from the reference program's by a relative error of at most 0.0065.
Values may be sent and summed in bfloat16 or wider, within the bound.
No kernel may reach another device: no remote copies, remote signals or barrier semaphores. Data moves between devices by JAX's collectives and lax.ppermute only.
A program may use at most 32 MiB of HBM per device.

```python
import math
import jax
import jax.numpy as jnp
import numpy as np
from jax import lax

D = 1024
FF = 768
TOP = 2
TOK_DEV = 128
EXPERTS = 8
CAP = 48
TOKENS = 131072
DEVICES = 1024


def steps_of(key, extent, shards, low, top_value):
    def one(position, blocks):
        draws = jax.random.uniform(jax.random.fold_in(jax.random.fold_in(key, 6), position), (blocks,), jnp.float32, low / len(shards), top_value / len(shards))
        return jnp.repeat(jnp.exp(draws), extent[position] // blocks).reshape((-1,) + (1,) * (len(extent) - position - 1))

    gain = one(*shards[0])
    for cut in shards[1:]:
        gain = gain * one(*cut)
    return gain


def shared_out(own_key, own, number, rows, number_of, top, most, skew):
    sequence = jax.random.permutation(own_key, number_of)
    packed, ordinary = load_shares(number_of, rows * top, most, skew, True), load_shares(number_of, rows * top, most, skew, False)
    places = jnp.arange(number_of)

    def named(sizes, offset_by):
        used = int((sizes > 0).sum())
        fixed = max(1, used // 4)
        passed = fixed + (places - fixed + offset_by * (used - fixed)) % max(1, number_of - fixed)
        return jnp.zeros((number_of,), jnp.int32).at[sequence[jnp.where(places < fixed, places, passed)]].set(jnp.asarray(sizes, jnp.int32))

    sizes = jnp.where(number % 4 == 0, named(packed, number // 4), named(ordinary, number - number // 4 - 1))
    mixed = jax.random.permutation(jax.random.fold_in(own, 3), number_of)
    source_of, taker = mixed[0:number_of // 2 * 2:2], mixed[1:number_of // 2 * 2:2]
    room = jnp.minimum(sizes[source_of] - 1, most - sizes[taker]) // 2
    room = jnp.where((source_of == sequence[0]) | (taker == sequence[0]) | (sizes[taker] == 0), 0, jnp.maximum(room, 0))
    passed = jax.random.randint(jax.random.fold_in(own, 4), (number_of // 2,), 0, 1 << 20) % (room + 1)
    sizes = sizes.at[source_of].add(-passed).at[taker].add(passed)
    items = jnp.searchsorted(jnp.cumsum(sizes), jnp.arange(rows * top), side="right").astype(jnp.int32)
    listing = items.reshape(top, rows).T
    listing = listing[jax.random.permutation(jax.random.fold_in(own, 1), rows)]
    offset_by = jax.random.randint(jax.random.fold_in(own, 2), (rows, 1), 0, top)
    return jnp.take_along_axis(listing, (jnp.arange(top)[None, :] + offset_by) % top, axis=1)


def load_shares(amount, total, most, slope, full):
    loads = [(1 << 20) // math.isqrt(grade ** slope) + 1 for grade in range(1, amount + 1)]
    largest = most if full else min(most, max(-(-total // amount), total * loads[0] // sum(loads)))
    least = 1 if total - largest >= amount - 1 else 0
    counts, surplus = [largest] + [least] * (amount - 1), total - largest - least * (amount - 1)
    while surplus > 0:
        movable = [i for i in range(1, amount) if counts[i] < largest] or [i for i in range(1, amount) if counts[i] < most]
        mass, budget = sum([loads[i] for i in movable]), surplus
        for i in movable:
            addition = min(most - counts[i], max(1, budget * loads[i] // mass), surplus)
            counts[i] = counts[i] + addition
            surplus = surplus - addition
    return np.array(counts)


def noise(key, dims, width, bound, shards=(), kind=jnp.bfloat16):
    array = jax.random.normal(key, dims, jnp.float32) * width
    if len(shards) > 0:
        array = steps_of(key, dims, shards, -0.22, 0.18) * array
    return jnp.clip(array, min=-bound, max=bound).astype(kind)


def setup_inputs(seed: int = 0) -> dict:
    seeds = jax.random.split(jax.random.key(seed), 8)
    tokens = noise(seeds[0], (TOKENS, D), 1.0, 6.0, ((0, 1024),))
    expert_ids_keys = jax.random.split(jax.random.fold_in(seeds[1], 1), TOKENS // TOK_DEV)
    expert_ids_turns = jax.random.permutation(jax.random.fold_in(seeds[1], 3), TOKENS // TOK_DEV)
    expert_ids = jax.vmap(lambda own, number: shared_out(jax.random.fold_in(seeds[1], 2), own, number, TOK_DEV, EXPERTS, TOP, CAP, 2))(expert_ids_keys, expert_ids_turns).reshape((TOKENS, TOP))
    combine = jnp.clip(0.2 + 0.8 * jax.random.uniform(seeds[2], (TOKENS, TOP), jnp.float32) ** steps_of(seeds[2], (TOKENS, TOP), ((0, 1024),), -0.2, 0.2), 0.2, 1.0)
    w_gate = noise(seeds[3], (EXPERTS, D, FF), D ** -0.5, 0.1875, ((0, 8), (1, 128)))
    w_up = noise(seeds[4], (EXPERTS, D, FF), D ** -0.5, 0.1875, ((0, 8), (1, 128)))
    w_down = noise(seeds[5], (EXPERTS, D, FF), FF ** -0.5, 0.21875, ((0, 8), (1, 128)))
    cotangent = noise(seeds[6], (TOKENS, D), 1.0, 6.0, ((0, 1024),))
    return dict(tokens=tokens, expert_ids=expert_ids, combine=combine, w_gate=w_gate, w_up=w_up, w_down=w_down, cotangent=cotangent)


def place_rows(expert_ids):
    flat_ids = expert_ids.reshape(-1)
    onehot = (flat_ids[:, None] == jnp.arange(EXPERTS, dtype=jnp.int32)[None, :]).astype(jnp.int32)
    before = jnp.cumsum(onehot, axis=0) - onehot
    ranks = jnp.sum(before * onehot, axis=1)
    return (flat_ids * CAP + ranks).astype(jnp.int32)


def expert_work(inputs):
    rows_in, grads_in, gate_w, up_w, down_w = inputs
    gate = jnp.dot(rows_in, gate_w, preferred_element_type=jnp.float32)
    up = jnp.dot(rows_in, up_w, preferred_element_type=jnp.float32)
    hidden = (jax.nn.silu(gate) * up).astype(jnp.bfloat16)
    out_rows = jnp.dot(hidden, down_w.T, preferred_element_type=jnp.float32).astype(jnp.bfloat16)
    hidden_grad = jnp.dot(grads_in, down_w, preferred_element_type=jnp.float32)
    sigma = jax.nn.sigmoid(gate)
    gate_grad = (hidden_grad * up * sigma * (1.0 + gate * (1.0 - sigma))).astype(jnp.bfloat16)
    up_grad = (hidden_grad * gate * sigma).astype(jnp.bfloat16)
    row_grad = jnp.dot(gate_grad, gate_w.T, preferred_element_type=jnp.float32)
    row_grad = row_grad + jnp.dot(up_grad, up_w.T, preferred_element_type=jnp.float32)
    return out_rows, row_grad.astype(jnp.bfloat16)


def reference(tokens, expert_ids, combine, w_gate, w_up, w_down, cotangent):
    slot_index = jax.vmap(place_rows)(expert_ids.reshape(DEVICES, TOK_DEV, TOP))
    device_rows = jnp.arange(DEVICES, dtype=jnp.int32)[:, None]
    token_copies = jnp.repeat(tokens, TOP, axis=0).reshape(DEVICES, TOK_DEV * TOP, D)
    scaled = (combine[:, :, None] * cotangent.astype(jnp.float32)[:, None, :]).astype(jnp.bfloat16)
    scaled = scaled.reshape(DEVICES, TOK_DEV * TOP, D)

    def pack(values):
        buffer = jnp.zeros((DEVICES, EXPERTS * CAP, D), jnp.bfloat16).at[device_rows, slot_index].set(values)
        return buffer.reshape(DEVICES, EXPERTS, CAP, D).transpose(1, 0, 2, 3).reshape(EXPERTS, DEVICES * CAP, D)

    def unpack(values):
        buffer = values.reshape(EXPERTS, DEVICES, CAP, D).transpose(1, 0, 2, 3).reshape(DEVICES, EXPERTS * CAP, D)
        return buffer[device_rows, slot_index].reshape(TOKENS, TOP, D)

    out_rows, row_grads = lax.map(expert_work, (pack(token_copies), pack(scaled), w_gate, w_up, w_down))
    expert_out = unpack(out_rows).astype(jnp.float32)
    row_grad = unpack(row_grads).astype(jnp.float32)
    mixed = jnp.sum(combine[:, :, None] * expert_out, axis=1).astype(jnp.bfloat16)
    combine_grad = jnp.sum(cotangent.astype(jnp.float32)[:, None, :] * expert_out, axis=2)
    input_grad = jnp.sum(row_grad, axis=1).astype(jnp.bfloat16)
    return mixed, input_grad, combine_grad
```

```python
import jax
import jax.numpy as jnp
from jax import lax
from jax.experimental import pallas as pl
from jax.experimental.pallas import tpu as pltpu
from jax.sharding import PartitionSpec as P

F32 = jnp.float32
BF16 = jnp.bfloat16
ALL = ("dp", "expert")
NY, CORES, PAR = 4, 2, 2


def call(body, name, out_shape, *args, mib=16):
    spec = pl.BlockSpec(memory_space=pltpu.VMEM)
    many = isinstance(out_shape, tuple)
    return pl.pallas_call(
        body,
        out_shape=out_shape,
        in_specs=[spec] * len(args),
        out_specs=(spec,) * len(out_shape) if many else spec,
        compiler_params=pltpu.CompilerParams(vmem_limit_bytes=mib * 1024 * 1024),
        name=name,
    )(*args)


def nt(left, right):
    return lax.dot_general(left, right, (((1,), (1,)), ((), ())), preferred_element_type=F32)


def nn(left, right):
    return jnp.dot(left, right, preferred_element_type=F32)


def pack_kernel(experts, ids_ref, comb_ref, tok_ref, cot_ref, sent_ref, grad_ref, pick_ref, ccol_ref):
    top, rows = ids_ref.shape
    slots = sent_ref.shape[0]
    capacity = slots // experts
    ids = ids_ref[...]
    kinds = lax.broadcasted_iota(jnp.int32, (experts, rows), 0)
    named = jnp.zeros((experts, rows), F32)
    for k in range(top):
        named = named + jnp.where(ids[k : k + 1, :] == kinds, 1.0, 0.0)
    earlier = jnp.where(
        lax.broadcasted_iota(jnp.int32, (rows, rows), 0)
        < lax.broadcasted_iota(jnp.int32, (rows, rows), 1),
        1.0,
        0.0,
    )
    before = nn(named.astype(BF16), earlier.astype(BF16))
    place = before + kinds.astype(F32) * capacity
    slot_iota = lax.broadcasted_iota(jnp.int32, (slots, rows), 0).astype(F32)
    spread = jnp.zeros((slots, rows), F32)
    weight = jnp.zeros((slots, rows), F32)
    for k in range(top):
        slot = jnp.sum(jnp.where(ids[k : k + 1, :] == kinds, place, 0.0), axis=0, keepdims=True)
        hot = jnp.where(slot_iota == slot, 1.0, 0.0)
        spread = spread + hot
        weight = weight + hot * comb_ref[k : k + 1, :]
        pick_ref[k] = jnp.transpose(hot).astype(BF16)
    spread = spread.astype(BF16)
    sent_ref[...] = nn(spread, tok_ref[...]).astype(BF16)
    cot_rows = nn(spread, cot_ref[...])
    grad_ref[...] = (cot_rows * jnp.sum(weight, axis=1, keepdims=True)).astype(BF16)
    padded = jnp.concatenate([comb_ref[...], jnp.zeros((rows - top, rows), F32)], axis=0)
    ccol_ref[...] = jnp.transpose(padded)


def order_kernel(zs, order_ref):
    width = order_ref.shape[0]
    dp = lax.axis_index("dp")
    core = lax.rem(lax.axis_index("expert"), CORES)
    my_z, my_y = dp // NY, lax.rem(dp, NY)
    depth = width // (zs * NY)
    i = lax.broadcasted_iota(jnp.int32, (1, width), 1)
    r = lax.rem(i, depth)
    pos = lax.rem(i // depth, zs // PAR)
    step = i // (depth * zs)
    other = lax.rem(i // (depth * (zs // PAR)), PAR)
    zi = jnp.where(core == 0, pos, zs // PAR - 1 - pos)
    y = lax.rem(jnp.where(core == 0, my_y + NY - step, my_y + step), NY)
    z = zi * PAR + lax.rem(my_z + other, PAR)
    feature = (z * NY + y) * depth + r
    tile = 128

    def one(t, carry):
        d = lax.broadcasted_iota(jnp.int32, (tile, width), 0) + t * tile
        order_ref[pl.ds(pl.multiple_of(t * tile, tile), tile), :] = jnp.where(
            d == feature, 1.0, 0.0
        ).astype(BF16)
        return carry

    lax.fori_loop(0, width // tile, one, 0)


def turn_kernel(rows_ref, order_ref, out_ref):
    out_ref[...] = nn(rows_ref[...], order_ref[...]).astype(BF16)


def pieces_dot(rows_ref, pieces, columns):
    start, total = 0, None
    for piece in pieces:
        size = piece.shape[0]
        part = nn(rows_ref[:, start : start + size], piece[:, columns])
        total = part if total is None else total + part
        start += size
    return total


def hidden_kernel(count, rows_ref, *refs):
    gates, ups = refs[:count], refs[count : 2 * count]
    hidden_ref, to_gate_ref, to_up_ref = refs[2 * count :]
    tile = 256
    for t in range(hidden_ref.shape[1] // tile):
        columns = slice(t * tile, (t + 1) * tile)
        gate = pieces_dot(rows_ref, gates, columns)
        up = pieces_dot(rows_ref, ups, columns)
        sigma = 1.0 / (1.0 + jnp.exp(-gate))
        silu = gate * sigma
        hidden_ref[:, columns] = (silu * up).astype(BF16)
        to_up_ref[:, columns] = silu
        to_gate_ref[:, columns] = up * sigma * (1.0 + gate * (1.0 - sigma))


def out_kernel(count, hidden_ref, order_ref, *refs):
    downs, out_ref, held_ref = refs[:count], refs[count], refs[count + 1]
    start = 0
    for piece in downs:
        size = piece.shape[0]
        held_ref[:, start : start + size] = nt(hidden_ref[...], piece[...]).astype(BF16)
        start += size
    out_ref[...] = nt(held_ref[...], order_ref[...]).astype(BF16)


def rows_kernel(count, grads_ref, to_gate_ref, to_up_ref, order_ref, *refs):
    gates, ups, downs = refs[:count], refs[count : 2 * count], refs[2 * count : 3 * count]
    out_ref, gate_grad_ref, up_grad_ref, held_ref = refs[3 * count :]
    tile = 256
    for t in range(to_up_ref.shape[1] // tile):
        columns = slice(t * tile, (t + 1) * tile)
        hidden_grad = pieces_dot(grads_ref, downs, columns)
        gate_grad_ref[:, columns] = (hidden_grad * to_gate_ref[:, columns]).astype(BF16)
        up_grad_ref[:, columns] = (hidden_grad * to_up_ref[:, columns]).astype(BF16)
    start = 0
    for gate, up in zip(gates, ups):
        size = gate.shape[0]
        total = nt(gate_grad_ref[...], gate[...]) + nt(up_grad_ref[...], up[...])
        held_ref[:, start : start + size] = total.astype(BF16)
        start += size
    out_ref[...] = nt(held_ref[...], order_ref[...]).astype(BF16)


def mixed_kernel(pick_ref, ccol_ref, cot_ref, back_ref, mixed_ref, cgrad_ref):
    top, rows, _ = pick_ref.shape
    cot = cot_ref[...].astype(F32)
    back = back_ref[...]
    lane = lax.broadcasted_iota(jnp.int32, (rows, rows), 1)
    mixed = jnp.zeros(cot.shape, F32)
    grads = jnp.zeros((rows, rows), F32)
    for k in range(top):
        out = nn(pick_ref[k], back)
        mixed = mixed + ccol_ref[:, k : k + 1] * out
        grads = jnp.where(lane == k, jnp.sum(cot * out, axis=1, keepdims=True), grads)
    mixed_ref[...] = mixed.astype(BF16)
    cgrad_ref[...] = jnp.transpose(grads)[:top, :]


def sum_kernel(pick_ref, back_ref, grad_ref):
    both = pick_ref[0]
    for k in range(1, pick_ref.shape[0]):
        both = both + pick_ref[k]
    grad_ref[...] = nn(both, back_ref[...]).astype(BF16)


def on_device(tokens, expert_ids, combine, w_gate, w_up, w_down, cotangent):
    groups = lax.axis_size("expert")
    zs = lax.axis_size("dp") // NY
    rows, top = expert_ids.shape
    width = tokens.shape[1]
    ff = w_gate.shape[2]
    capacity = 3 * rows * top // (2 * groups)
    slots = groups * capacity
    shape = jax.ShapeDtypeStruct

    def device(z, y, e):
        return ((z % zs) * NY + y % NY) * groups + e

    def shifted(dz, dy):
        return [
            (device(z, y, e), device(z + s * dz, y + s * dy, e))
            for z in range(zs)
            for y in range(NY)
            for e in range(groups)
            for s in ((1, -1)[e % CORES],)
        ]

    far_groups = [
        [device(z, y, e) for z in range(par, zs, PAR)][:: (1, -1)[e % CORES]]
        for par in range(PAR)
        for y in range(NY)
        for e in range(groups)
    ]
    near_perm, y_perm = shifted(1, 0), shifted(0, 1)

    def swap(values):
        split = values.reshape(groups, capacity, width)
        return lax.all_to_all(split, "expert", 0, 0, tiled=True).reshape(slots, width)

    joined = jnp.concatenate([w_gate[0], w_up[0], w_down[0]], axis=1)
    far = lax.all_gather(joined, ALL, axis=0, tiled=True, axis_index_groups=far_groups)
    sent_tokens, sent_grads, pick, ccol = call(
        lambda *refs: pack_kernel(groups, *refs),
        "pack",
        (
            shape((slots, width), BF16),
            shape((slots, width), BF16),
            shape((top, rows, slots), BF16),
            shape((rows, rows), F32),
        ),
        expert_ids.T,
        combine.T,
        tokens,
        cotangent,
    )
    order = call(lambda ref: order_kernel(zs, ref), "order", shape((width, width), BF16))
    arrived = swap(sent_tokens)
    arrived_grads = swap(sent_grads)
    kept = [far[:, m * ff : (m + 1) * ff] for m in range(3)]
    near = [lax.ppermute(k, ALL, near_perm) for k in kept]
    pieces = [[jnp.concatenate([k, n], axis=0)] for k, n in zip(kept, near)]
    for _ in range(NY - 1):
        for held in pieces:
            held.append(lax.ppermute(held[-1], ALL, y_perm))
    gates, ups, downs = pieces
    count = len(gates)
    turned = call(turn_kernel, "turn", shape((slots, width), BF16), arrived, order)
    turned_grads = call(turn_kernel, "turn", shape((slots, width), BF16), arrived_grads, order)
    hidden, to_gate, to_up = call(
        lambda *refs: hidden_kernel(count, *refs),
        "hidden",
        (shape((slots, ff), BF16), shape((slots, ff), F32), shape((slots, ff), F32)),
        turned,
        *gates,
        *ups,
        mib=20,
    )
    spec = pl.BlockSpec(memory_space=pltpu.VMEM)
    out_rows = pl.pallas_call(
        lambda *refs: out_kernel(count, *refs),
        out_shape=shape((slots, width), BF16),
        in_specs=[spec] * (2 + count),
        out_specs=spec,
        scratch_shapes=[pltpu.VMEM((slots, width), BF16)],
        compiler_params=pltpu.CompilerParams(vmem_limit_bytes=16 * 1024 * 1024),
        name="out_rows",
    )(hidden, order, *downs)
    back_out = swap(out_rows)
    row_grads = pl.pallas_call(
        lambda *refs: rows_kernel(count, *refs),
        out_shape=shape((slots, width), BF16),
        in_specs=[spec] * (4 + 3 * count),
        out_specs=spec,
        scratch_shapes=[
            pltpu.VMEM((slots, ff), BF16),
            pltpu.VMEM((slots, ff), BF16),
            pltpu.VMEM((slots, width), BF16),
        ],
        compiler_params=pltpu.CompilerParams(vmem_limit_bytes=24 * 1024 * 1024),
        name="row_grads",
    )(turned_grads, to_gate, to_up, order, *gates, *ups, *downs)
    back_grad = swap(row_grads)
    mixed, combine_grad = call(
        mixed_kernel,
        "mixed",
        (shape((rows, width), BF16), shape((top, rows), F32)),
        pick,
        ccol,
        cotangent,
        back_out,
    )
    input_grad = call(sum_kernel, "summed", shape((rows, width), BF16), pick, back_grad)
    return mixed, input_grad, combine_grad.T


def solution(mesh):
    rows = P(ALL, None)
    weights = P("expert", "dp", None)
    return jax.shard_map(
        on_device,
        mesh=mesh,
        in_specs=(rows, rows, rows, weights, weights, weights, rows),
        out_specs=(rows, rows, rows),
        check_vma=False,
    )
```

```python
import jax
import jax.numpy as jnp
from jax import lax
from jax.experimental import pallas as pl
from jax.experimental.pallas import tpu as pltpu
from jax.sharding import PartitionSpec as P

F32 = jnp.float32
BF16 = jnp.bfloat16
ALL = ("dp", "expert")
NY, CORES, PAR = 4, 2, 2


def call(body, name, out_shape, *args, mib=16):
    spec = pl.BlockSpec(memory_space=pltpu.VMEM)
    many = isinstance(out_shape, tuple)
    return pl.pallas_call(
        body,
        out_shape=out_shape,
        in_specs=[spec] * len(args),
        out_specs=(spec,) * len(out_shape) if many else spec,
        compiler_params=pltpu.CompilerParams(vmem_limit_bytes=mib * 1024 * 1024),
        name=name,
    )(*args)


def nt(left, right):
    return lax.dot_general(left, right, (((1,), (1,)), ((), ())), preferred_element_type=F32)


def nn(left, right):
    return jnp.dot(left, right, preferred_element_type=F32)


def places(ids, experts, capacity):
    top, rows = ids.shape
    kinds = lax.broadcasted_iota(jnp.int32, (experts, rows), 0)
    named = jnp.zeros((experts, rows), F32)
    for k in range(top):
        named = named + jnp.where(ids[k : k + 1, :] == kinds, 1.0, 0.0)
    earlier = jnp.where(
        lax.broadcasted_iota(jnp.int32, (rows, rows), 0)
        < lax.broadcasted_iota(jnp.int32, (rows, rows), 1),
        1.0,
        0.0,
    )
    before = nn(named.astype(BF16), earlier.astype(BF16))
    place = before + kinds.astype(F32) * capacity
    return [
        jnp.sum(jnp.where(ids[k : k + 1, :] == kinds, place, 0.0), axis=0, keepdims=True)
        for k in range(top)
    ]


def pack_kernel(ids_ref, comb_ref, tok_ref, cot_ref, sent_ref, held_ref, sems):
    top, rows = ids_ref.shape
    experts, capacity = sent_ref.shape[0], sent_ref.shape[1] // 2
    slots = experts * capacity
    slot_iota = lax.broadcasted_iota(jnp.int32, (slots, rows), 0).astype(F32)
    spread = jnp.zeros((slots, rows), F32)
    weight = jnp.zeros((slots, rows), F32)
    for k, slot in enumerate(places(ids_ref[...], experts, capacity)):
        hot = jnp.where(slot_iota == slot, 1.0, 0.0)
        spread = spread + hot
        weight = weight + hot * comb_ref[k : k + 1, :]
    spread = spread.astype(BF16)
    put_rows(held_ref, 0, nn(spread, tok_ref[...]).astype(BF16))
    first = send_out(held_ref, sent_ref, sems, 0)
    cot_rows = nn(spread, cot_ref[...])
    put_rows(held_ref, 1, (cot_rows * jnp.sum(weight, axis=1, keepdims=True)).astype(BF16))
    second = send_out(held_ref, sent_ref, sems, 1)
    first.wait()
    second.wait()


def put_rows(held_ref, half, values, columns=slice(None)):
    experts, capacity = held_ref.shape[0], held_ref.shape[1] // 2
    for e in range(experts):
        held_ref[e, half * capacity : (half + 1) * capacity, columns] = values[
            e * capacity : (e + 1) * capacity
        ]


def take_rows(ref, half):
    experts, capacity = ref.shape[0], ref.shape[1] // 2
    return jnp.concatenate(
        [ref[e, half * capacity : (half + 1) * capacity] for e in range(experts)], axis=0
    )


def send_out(held_ref, out_ref, sems, half):
    capacity = held_ref.shape[1] // 2
    part = pl.ds(half * capacity, capacity)
    copy = pltpu.make_async_copy(held_ref.at[:, part], out_ref.at[:, part], sems.at[half])
    copy.start()
    return copy


def pick_kernel(experts, capacity, ids_ref, comb_ref, late_ref, pick_ref, ccol_ref):
    del late_ref
    top, rows = ids_ref.shape
    slots = experts * capacity
    slot_iota = lax.broadcasted_iota(jnp.int32, (slots, rows), 0).astype(F32)
    for k, slot in enumerate(places(ids_ref[...], experts, capacity)):
        pick_ref[k] = jnp.transpose(jnp.where(slot_iota == slot, 1.0, 0.0)).astype(BF16)
    padded = jnp.concatenate([comb_ref[...], jnp.zeros((rows - top, rows), F32)], axis=0)
    ccol_ref[...] = jnp.transpose(padded)


def order_kernel(zs, order_ref):
    width = order_ref.shape[0]
    dp = lax.axis_index("dp")
    core = lax.rem(lax.axis_index("expert"), CORES)
    my_z, my_y = dp // NY, lax.rem(dp, NY)
    depth = width // (zs * NY)
    i = lax.broadcasted_iota(jnp.int32, (1, width), 1)
    r = lax.rem(i, depth)
    pos = lax.rem(i // depth, zs // PAR)
    step = i // (depth * zs)
    other = lax.rem(i // (depth * (zs // PAR)), PAR)
    zi = jnp.where(core == 0, pos, zs // PAR - 1 - pos)
    ahead = jnp.where(step == 1, -1, jnp.where(step == 2, 1, step - step // 3))
    y = lax.rem(my_y + NY + jnp.where(core == 0, ahead, -ahead), NY)
    z = zi * PAR + lax.rem(my_z + other, PAR)
    feature = (z * NY + y) * depth + r
    tile = 128

    def one(t, carry):
        d = lax.broadcasted_iota(jnp.int32, (tile, width), 0) + t * tile
        order_ref[pl.ds(pl.multiple_of(t * tile, tile), tile), :] = jnp.where(
            d == feature, 1.0, 0.0
        ).astype(BF16)
        return carry

    lax.fori_loop(0, width // tile, one, 0)


def turn_kernel(rows_ref, order_ref, tok_ref, grad_ref):
    tok_ref[...] = nn(take_rows(rows_ref, 0), order_ref[...]).astype(BF16)
    grad_ref[...] = nn(take_rows(rows_ref, 1), order_ref[...]).astype(BF16)


def pair(pieces, columns):
    return jnp.concatenate([piece[:, columns] for piece in pieces], axis=0)


def partial_kernel(tok_ref, grad_ref, *refs):
    pieces, sums = refs[:-3], refs[-3:]
    ff = sums[0].shape[1]
    tile, depth = 256, 2 * pieces[0].shape[0]
    for m, (out_ref, rows_ref) in enumerate(zip(sums, (tok_ref, tok_ref, grad_ref))):
        for t in range(ff // tile):
            columns = slice(m * ff + t * tile, m * ff + (t + 1) * tile)
            total = None
            for j in range(len(pieces) // 2):
                part = nn(
                    rows_ref[:, j * depth : (j + 1) * depth],
                    pair(pieces[2 * j : 2 * j + 2], columns),
                )
                total = part if total is None else total + part
            out_ref[:, t * tile : (t + 1) * tile] = total


def final_kernel(count, tok_ref, grad_ref, order_ref, *refs):
    sums, pieces = refs[:3], refs[3 : 3 + count]
    out_ref, late_ref, hidden_ref, gate_grad_ref, up_grad_ref, arr_ref, held_ref, sems = refs[3 + count :]
    late_ref[...] = jnp.zeros_like(late_ref)
    ff, width = hidden_ref.shape[1], order_ref.shape[0]
    tile, depth = 256, 2 * pieces[0].shape[0]
    last = slice(width - depth, width)
    for t in range(ff // tile):
        here = slice(t * tile, (t + 1) * tile)
        gate, up, hidden_grad = (
            sums[m][:, here]
            + nn(rows_ref[:, last], pair(pieces[-2:], slice(m * ff + t * tile, m * ff + (t + 1) * tile)))
            for m, rows_ref in enumerate((tok_ref, tok_ref, grad_ref))
        )
        sigma = 1.0 / (1.0 + jnp.exp(-gate))
        silu = gate * sigma
        hidden_ref[:, here] = (silu * up).astype(BF16)
        up_grad_ref[:, here] = (hidden_grad * silu).astype(BF16)
        gate_grad_ref[:, here] = (hidden_grad * up * sigma * (1.0 + gate * (1.0 - sigma))).astype(BF16)
    copies = []
    for half, terms in enumerate((((hidden_ref, 2),), ((gate_grad_ref, 0), (up_grad_ref, 1)))):
        for j in range(count // 2):
            total = None
            for left_ref, m in terms:
                part = nt(left_ref[...], pair(pieces[2 * j : 2 * j + 2], slice(m * ff, (m + 1) * ff)))
                total = part if total is None else total + part
            arr_ref[half, :, j * depth : (j + 1) * depth] = total.astype(BF16)
        for t in range(width // tile):
            here = slice(t * tile, (t + 1) * tile)
            put_rows(held_ref, half, nt(arr_ref[half], order_ref[here, :]).astype(BF16), here)
        copies.append(send_out(held_ref, out_ref, sems, half))
    for copy in copies:
        copy.wait()


def post_kernel(pick_ref, ccol_ref, cot_ref, back_ref, mixed_ref, igrad_ref, cgrad_ref):
    top, rows, _ = pick_ref.shape
    cot = cot_ref[...].astype(F32)
    back = take_rows(back_ref, 0)
    lane = lax.broadcasted_iota(jnp.int32, (rows, rows), 1)
    mixed = jnp.zeros(cot.shape, F32)
    grads = jnp.zeros((rows, rows), F32)
    both = None
    for k in range(top):
        out = nn(pick_ref[k], back)
        mixed = mixed + ccol_ref[:, k : k + 1] * out
        grads = jnp.where(lane == k, jnp.sum(cot * out, axis=1, keepdims=True), grads)
        both = pick_ref[k] if both is None else both + pick_ref[k]
    mixed_ref[...] = mixed.astype(BF16)
    cgrad_ref[...] = jnp.transpose(grads)[:top, :]
    igrad_ref[...] = nn(both, take_rows(back_ref, 1)).astype(BF16)


def on_device(tokens, expert_ids, combine, w_gate, w_up, w_down, cotangent):
    groups = lax.axis_size("expert")
    zs = lax.axis_size("dp") // NY
    rows, top = expert_ids.shape
    width = tokens.shape[1]
    ff = w_gate.shape[2]
    capacity = 3 * rows * top // (2 * groups)
    slots = groups * capacity
    shape = jax.ShapeDtypeStruct

    def device(z, y, e):
        return ((z % zs) * NY + y % NY) * groups + e

    def shifted(dz, dy):
        return [
            (device(z, y, e), device(z + s * dz, y + s * dy, e))
            for z in range(zs)
            for y in range(NY)
            for e in range(groups)
            for s in ((1, -1)[e % CORES],)
        ]

    far_groups = [
        [device(z, y, e) for z in range(par, zs, PAR)][:: (1, -1)[e % CORES]]
        for par in range(PAR)
        for y in range(NY)
        for e in range(groups)
    ]

    def swap(values):
        return lax.all_to_all(values, "expert", 0, 0, tiled=True)

    def send(values, dz, dy):
        return lax.ppermute(values, ALL, shifted(dz, dy))

    joined = jnp.concatenate([w_gate[0], w_up[0], w_down[0]], axis=1)
    own = lax.all_gather(joined, ALL, axis=0, tiled=True, axis_index_groups=far_groups)
    ahead, behind = send(own, 0, 1), send(own, 0, -1)
    by_y = [own, ahead, behind, send(ahead, 0, 1)]
    pieces = [p for held in by_y for p in (held, send(held, 1, 0))]
    count = len(pieces)
    spec = pl.BlockSpec(memory_space=pltpu.VMEM)
    far_out = pl.BlockSpec(memory_space=pltpu.HBM)
    both = shape((groups, 2 * capacity, width), BF16)
    ids, weights = expert_ids.T, combine.T
    sent = pl.pallas_call(
        pack_kernel,
        out_shape=both,
        in_specs=[spec] * 4,
        out_specs=far_out,
        scratch_shapes=[pltpu.VMEM(both.shape, BF16), pltpu.SemaphoreType.DMA((2,))],
        compiler_params=pltpu.CompilerParams(vmem_limit_bytes=16 * 1024 * 1024),
        name="pack",
    )(ids, weights, tokens, cotangent)
    order = call(lambda ref: order_kernel(zs, ref), "order", shape((width, width), BF16))
    rows_shape, sum_shape = shape((slots, width), BF16), shape((slots, ff), F32)
    turned = call(turn_kernel, "turn", (rows_shape,) * 2, swap(sent), order)
    sums = call(partial_kernel, "partial", (sum_shape,) * 3, *turned, *pieces[:-2], mib=12)
    results, late = pl.pallas_call(
        lambda *refs: final_kernel(count, *refs),
        out_shape=(both, shape((8, 128), F32)),
        in_specs=[spec] * (6 + count),
        out_specs=(far_out, spec),
        scratch_shapes=[pltpu.VMEM((slots, ff), BF16)] * 3
        + [
            pltpu.VMEM((2, slots, width), BF16),
            pltpu.VMEM(both.shape, BF16),
            pltpu.SemaphoreType.DMA((2,)),
        ],
        compiler_params=pltpu.CompilerParams(vmem_limit_bytes=20 * 1024 * 1024),
        name="final",
    )(*turned, order, *sums, *pieces)
    back = swap(results)
    pick, ccol = pl.pallas_call(
        lambda *refs: pick_kernel(groups, capacity, *refs),
        out_shape=(shape((top, rows, slots), BF16), shape((rows, rows), F32)),
        in_specs=[spec] * 3,
        out_specs=(spec,) * 2,
        compiler_params=pltpu.CompilerParams(vmem_limit_bytes=8 * 1024 * 1024),
        name="pick",
    )(ids, weights, late)
    mixed, input_grad, combine_grad = call(
        post_kernel,
        "post",
        (shape((rows, width), BF16),) * 2 + (shape((top, rows), F32),),
        pick,
        ccol,
        cotangent,
        back,
    )
    return mixed, input_grad, combine_grad.T


def solution(mesh):
    rows = P(ALL, None)
    weights = P("expert", "dp", None)
    return jax.shard_map(
        on_device,
        mesh=mesh,
        in_specs=(rows, rows, rows, weights, weights, weights, rows),
        out_specs=(rows, rows, rows),
        check_vma=False,
    )
```

```python
import jax
import jax.numpy as jnp
from jax import lax
from jax.experimental import pallas as pl
from jax.experimental.pallas import tpu as pltpu
from jax.sharding import PartitionSpec as P

F32 = jnp.float32
BF16 = jnp.bfloat16
ALL = ("dp", "expert")
NY, CORES, PAR = 4, 2, 2


def call(body, name, out_shape, *args, mib=16):
    spec = pl.BlockSpec(memory_space=pltpu.VMEM)
    many = isinstance(out_shape, tuple)
    return pl.pallas_call(
        body,
        out_shape=out_shape,
        in_specs=[spec] * len(args),
        out_specs=(spec,) * len(out_shape) if many else spec,
        compiler_params=pltpu.CompilerParams(vmem_limit_bytes=mib * 1024 * 1024),
        name=name,
    )(*args)


def after(values, earlier):
    anywhere = pl.BlockSpec(memory_space=pl.ANY)
    return pl.pallas_call(
        lambda *refs: None,
        out_shape=jax.ShapeDtypeStruct(values.shape, values.dtype),
        in_specs=[anywhere] * 2,
        out_specs=anywhere,
        input_output_aliases={0: 0},
        compiler_params=pltpu.CompilerParams(vmem_limit_bytes=1024 * 1024),
        name="after",
    )(values, earlier)


def nt(left, right):
    return lax.dot_general(left, right, (((1,), (1,)), ((), ())), preferred_element_type=F32)


def nn(left, right):
    return jnp.dot(left, right, preferred_element_type=F32)


def places(ids, experts, capacity):
    top, rows = ids.shape
    kinds = lax.broadcasted_iota(jnp.int32, (experts, rows), 0)
    named = jnp.zeros((experts, rows), F32)
    for k in range(top):
        named = named + jnp.where(ids[k : k + 1, :] == kinds, 1.0, 0.0)
    earlier = jnp.where(
        lax.broadcasted_iota(jnp.int32, (rows, rows), 0)
        < lax.broadcasted_iota(jnp.int32, (rows, rows), 1),
        1.0,
        0.0,
    )
    before = nn(named.astype(BF16), earlier.astype(BF16))
    place = before + kinds.astype(F32) * capacity
    return [
        jnp.sum(jnp.where(ids[k : k + 1, :] == kinds, place, 0.0), axis=0, keepdims=True)
        for k in range(top)
    ]


def pack_kernel(*refs):
    sources, (sent_ref, joined_ref), targets = refs[:7], refs[7:9], refs[9:16]
    ids_ref, comb_ref, tok_ref, cot_ref = targets[3:]
    held_ref, sems, load_sems = refs[16:]
    loads = [
        pltpu.make_async_copy(source, target, load_sems.at[n])
        for n, (source, target) in enumerate(zip(sources, targets))
    ]
    for load in loads:
        load.start()
    ff = joined_ref.shape[1] // 3
    for m, load in enumerate(loads[:3]):
        load.wait()
        joined_ref[:, m * ff : (m + 1) * ff] = targets[m][0]
    loads = loads[3:]
    top, rows = ids_ref.shape
    experts, capacity = sent_ref.shape[0], sent_ref.shape[1] // 2
    slots = experts * capacity
    slot_iota = lax.broadcasted_iota(jnp.int32, (slots, rows), 0).astype(F32)
    spread = jnp.zeros((slots, rows), F32)
    weight = jnp.zeros((slots, rows), F32)
    loads[0].wait()
    loads[1].wait()
    for k, slot in enumerate(places(ids_ref[...], experts, capacity)):
        hot = jnp.where(slot_iota == slot, 1.0, 0.0)
        spread = spread + hot
        weight = weight + hot * comb_ref[k : k + 1, :]
    spread = spread.astype(BF16)
    loads[2].wait()
    put_rows(held_ref, 0, nn(spread, tok_ref[...]).astype(BF16))
    first = send_out(held_ref, sent_ref, sems, 0)
    loads[3].wait()
    cot_rows = nn(spread, cot_ref[...])
    put_rows(held_ref, 1, (cot_rows * jnp.sum(weight, axis=1, keepdims=True)).astype(BF16))
    second = send_out(held_ref, sent_ref, sems, 1)
    first.wait()
    second.wait()


def put_rows(held_ref, half, values, columns=slice(None)):
    experts, capacity = held_ref.shape[0], held_ref.shape[1] // 2
    for e in range(experts):
        held_ref[e, half * capacity : (half + 1) * capacity, columns] = values[
            e * capacity : (e + 1) * capacity
        ]


def take_rows(ref, half):
    experts, capacity = ref.shape[0], ref.shape[1] // 2
    return jnp.concatenate(
        [ref[e, half * capacity : (half + 1) * capacity] for e in range(experts)], axis=0
    )


def send_out(held_ref, out_ref, sems, half):
    capacity = held_ref.shape[1] // 2
    part = pl.ds(half * capacity, capacity)
    copy = pltpu.make_async_copy(held_ref.at[:, part], out_ref.at[:, part], sems.at[half])
    copy.start()
    return copy


def pick_kernel(experts, capacity, ids_ref, comb_ref, late_ref, pick_ref, ccol_ref):
    del late_ref
    top, rows = ids_ref.shape
    slots = experts * capacity
    slot_iota = lax.broadcasted_iota(jnp.int32, (slots, rows), 0).astype(F32)
    for k, slot in enumerate(places(ids_ref[...], experts, capacity)):
        pick_ref[k] = jnp.transpose(jnp.where(slot_iota == slot, 1.0, 0.0)).astype(BF16)
    padded = jnp.concatenate([comb_ref[...], jnp.zeros((rows - top, rows), F32)], axis=0)
    ccol_ref[...] = jnp.transpose(padded)


def order_kernel(zs, order_ref):
    width = order_ref.shape[0]
    dp = lax.axis_index("dp")
    core = lax.rem(lax.axis_index("expert"), CORES)
    my_z, my_y = dp // NY, lax.rem(dp, NY)
    depth = width // (zs * NY)
    i = lax.broadcasted_iota(jnp.int32, (1, width), 1)
    r = lax.rem(i, depth)
    pos = lax.rem(i // depth, zs // PAR)
    step = i // (depth * zs)
    other = lax.rem(i // (depth * (zs // PAR)), PAR)
    zi = jnp.where(core == 0, pos, zs // PAR - 1 - pos)
    ahead = jnp.where(step == 1, -1, jnp.where(step == 2, 1, step - step // 3))
    y = lax.rem(my_y + NY + jnp.where(core == 0, ahead, -ahead), NY)
    z = zi * PAR + lax.rem(my_z + other, PAR)
    feature = (z * NY + y) * depth + r
    tile = 128

    def one(t, carry):
        d = lax.broadcasted_iota(jnp.int32, (tile, width), 0) + t * tile
        order_ref[pl.ds(pl.multiple_of(t * tile, tile), tile), :] = jnp.where(
            d == feature, 1.0, 0.0
        ).astype(BF16)
        return carry

    lax.fori_loop(0, width // tile, one, 0)


def turn_kernel(rows_ref, order_ref, tok_ref, grad_ref):
    tok_ref[...] = nn(take_rows(rows_ref, 0), order_ref[...]).astype(BF16)
    grad_ref[...] = nn(take_rows(rows_ref, 1), order_ref[...]).astype(BF16)


def pair(pieces, columns):
    return jnp.concatenate([piece[:, columns] for piece in pieces], axis=0)


def partial_kernel(tok_ref, grad_ref, *refs):
    pieces, sums = refs[:-3], refs[-3:]
    ff = sums[0].shape[1]
    tile, depth = 256, 2 * pieces[0].shape[0]
    for m, (out_ref, rows_ref) in enumerate(zip(sums, (tok_ref, tok_ref, grad_ref))):
        for t in range(ff // tile):
            columns = slice(m * ff + t * tile, m * ff + (t + 1) * tile)
            total = None
            for j in range(len(pieces) // 2):
                part = nn(
                    rows_ref[:, j * depth : (j + 1) * depth],
                    pair(pieces[2 * j : 2 * j + 2], columns),
                )
                total = part if total is None else total + part
            out_ref[:, t * tile : (t + 1) * tile] = total


def final_kernel(count, tok_ref, grad_ref, order_ref, *refs):
    sums, pieces = refs[:3], refs[3 : 3 + count]
    out_ref, late_ref, hidden_ref, gate_grad_ref, up_grad_ref, arr_ref, held_ref, sems = refs[3 + count :]
    late_ref[...] = jnp.zeros_like(late_ref)
    ff, width = hidden_ref.shape[1], order_ref.shape[0]
    tile, depth = 256, 2 * pieces[0].shape[0]
    last = slice(width - depth, width)
    for t in range(ff // tile):
        here = slice(t * tile, (t + 1) * tile)
        gate, up, hidden_grad = (
            sums[m][:, here]
            + nn(rows_ref[:, last], pair(pieces[-2:], slice(m * ff + t * tile, m * ff + (t + 1) * tile)))
            for m, rows_ref in enumerate((tok_ref, tok_ref, grad_ref))
        )
        sigma = 1.0 / (1.0 + jnp.exp(-gate))
        silu = gate * sigma
        hidden_ref[:, here] = (silu * up).astype(BF16)
        up_grad_ref[:, here] = (hidden_grad * silu).astype(BF16)
        gate_grad_ref[:, here] = (hidden_grad * up * sigma * (1.0 + gate * (1.0 - sigma))).astype(BF16)
    copies = []
    for half, terms in enumerate((((hidden_ref, 2),), ((gate_grad_ref, 0), (up_grad_ref, 1)))):
        for j in range(count // 2):
            total = None
            for left_ref, m in terms:
                part = nt(left_ref[...], pair(pieces[2 * j : 2 * j + 2], slice(m * ff, (m + 1) * ff)))
                total = part if total is None else total + part
            arr_ref[half, :, j * depth : (j + 1) * depth] = total.astype(BF16)
        for t in range(width // tile):
            here = slice(t * tile, (t + 1) * tile)
            put_rows(held_ref, half, nt(arr_ref[half], order_ref[here, :]).astype(BF16), here)
        copies.append(send_out(held_ref, out_ref, sems, half))
    for copy in copies:
        copy.wait()


def post_kernel(pick_ref, ccol_ref, cot_ref, back_ref, mixed_ref, igrad_ref, cgrad_ref):
    top, rows, _ = pick_ref.shape
    cot = cot_ref[...].astype(F32)
    back = take_rows(back_ref, 0)
    lane = lax.broadcasted_iota(jnp.int32, (rows, rows), 1)
    mixed = jnp.zeros(cot.shape, F32)
    grads = jnp.zeros((rows, rows), F32)
    both = None
    for k in range(top):
        out = nn(pick_ref[k], back)
        mixed = mixed + ccol_ref[:, k : k + 1] * out
        grads = jnp.where(lane == k, jnp.sum(cot * out, axis=1, keepdims=True), grads)
        both = pick_ref[k] if both is None else both + pick_ref[k]
    mixed_ref[...] = mixed.astype(BF16)
    cgrad_ref[...] = jnp.transpose(grads)[:top, :]
    igrad_ref[...] = nn(both, take_rows(back_ref, 1)).astype(BF16)


def on_device(tokens, expert_ids, combine, w_gate, w_up, w_down, cotangent):
    groups = lax.axis_size("expert")
    zs = lax.axis_size("dp") // NY
    rows, top = expert_ids.shape
    width = tokens.shape[1]
    ff = w_gate.shape[2]
    capacity = 3 * rows * top // (2 * groups)
    slots = groups * capacity
    shape = jax.ShapeDtypeStruct

    def device(z, y, e):
        return ((z % zs) * NY + y % NY) * groups + e

    def shifted(dz, dy):
        return [
            (device(z, y, e), device(z + s * dz, y + s * dy, e))
            for z in range(zs)
            for y in range(NY)
            for e in range(groups)
            for s in ((1, -1)[e % CORES],)
        ]

    far_groups = [
        [device(z, y, e) for z in range(par, zs, PAR)][:: (1, -1)[e % CORES]]
        for par in range(PAR)
        for y in range(NY)
        for e in range(groups)
    ]

    def swap(values):
        return lax.all_to_all(values, "expert", 0, 0, tiled=True)

    def send(values, dz, dy):
        return lax.ppermute(values, ALL, shifted(dz, dy))

    spec = pl.BlockSpec(memory_space=pltpu.VMEM)
    both = shape((groups, 2 * capacity, width), BF16)
    ids, weights = expert_ids.T, combine.T
    depth = w_gate.shape[1]
    hbm = pl.BlockSpec(memory_space=pltpu.HBM)
    sources = (w_gate, w_up, w_down, ids, weights, tokens, cotangent)
    sent, joined = pl.pallas_call(
        pack_kernel,
        out_shape=(both, shape((depth, 3 * ff), BF16)),
        in_specs=[hbm] * len(sources),
        out_specs=(hbm, spec),
        scratch_shapes=[pltpu.VMEM(v.shape, v.dtype) for v in sources]
        + [
            pltpu.VMEM(both.shape, BF16),
            pltpu.SemaphoreType.DMA((2,)),
            pltpu.SemaphoreType.DMA((len(sources),)),
        ],
        compiler_params=pltpu.CompilerParams(vmem_limit_bytes=12 * 1024 * 1024),
        name="pack",
    )(*(pltpu.with_memory_space_constraint(v, pltpu.HBM) for v in sources))
    arrived = swap(sent)
    own = lax.all_gather(joined, ALL, axis=0, tiled=True, axis_index_groups=far_groups)
    own = after(own, arrived)
    ahead, beside, behind = send(own, 0, 1), send(own, 1, 0), send(own, 0, -1)
    across = send(ahead, 0, 1)
    pieces = [own, beside, ahead, send(ahead, 1, 0), behind, send(beside, 0, -1)]
    pieces += [across, send(across, 1, 0)]
    count = len(pieces)
    order = call(lambda ref: order_kernel(zs, ref), "order", shape((width, width), BF16))
    rows_shape, sum_shape = shape((slots, width), BF16), shape((slots, ff), F32)
    turned = call(turn_kernel, "turn", (rows_shape,) * 2, arrived, order)
    sums = call(partial_kernel, "partial", (sum_shape,) * 3, *turned, *pieces[:-2], mib=12)
    results, late = pl.pallas_call(
        lambda *refs: final_kernel(count, *refs),
        out_shape=(pltpu.HBM(both.shape, BF16), shape((8, 128), F32)),
        in_specs=[spec] * (6 + count),
        out_specs=(hbm, spec),
        scratch_shapes=[pltpu.VMEM((slots, ff), BF16)] * 3
        + [
            pltpu.VMEM((2, slots, width), BF16),
            pltpu.VMEM(both.shape, BF16),
            pltpu.SemaphoreType.DMA((2,)),
        ],
        compiler_params=pltpu.CompilerParams(vmem_limit_bytes=20 * 1024 * 1024),
        name="final",
    )(*turned, order, *sums, *pieces)
    back = swap(results)
    pick, ccol = pl.pallas_call(
        lambda *refs: pick_kernel(groups, capacity, *refs),
        out_shape=(shape((top, rows, slots), BF16), shape((rows, rows), F32)),
        in_specs=[spec] * 3,
        out_specs=(spec,) * 2,
        compiler_params=pltpu.CompilerParams(vmem_limit_bytes=8 * 1024 * 1024),
        name="pick",
    )(ids, weights, late)
    mixed, input_grad, combine_grad = call(
        post_kernel,
        "post",
        (shape((rows, width), BF16),) * 2 + (shape((top, rows), F32),),
        pick,
        ccol,
        cotangent,
        back,
    )
    return mixed, input_grad, combine_grad.T


def solution(mesh):
    rows = P(ALL, None)
    weights = P("expert", "dp", None)
    return jax.shard_map(
        on_device,
        mesh=mesh,
        in_specs=(rows, rows, rows, weights, weights, weights, rows),
        out_specs=(rows, rows, rows),
        check_vma=False,
    )
```

```python
import jax
import jax.numpy as jnp
from jax import lax
from jax.experimental import pallas as pl
from jax.experimental.pallas import tpu as pltpu
from jax.sharding import PartitionSpec as P

F32 = jnp.float32
BF16 = jnp.bfloat16
ALL = ("dp", "expert")
NY, CORES, PAR = 4, 2, 2


def call(body, name, out_shape, *args, mib=16):
    spec = pl.BlockSpec(memory_space=pltpu.VMEM)
    many = isinstance(out_shape, tuple)
    return pl.pallas_call(
        body,
        out_shape=out_shape,
        in_specs=[spec] * len(args),
        out_specs=(spec,) * len(out_shape) if many else spec,
        compiler_params=pltpu.CompilerParams(vmem_limit_bytes=mib * 1024 * 1024),
        name=name,
    )(*args)


def after(values, earlier):
    anywhere = pl.BlockSpec(memory_space=pl.ANY)
    return pl.pallas_call(
        lambda *refs: None,
        out_shape=jax.ShapeDtypeStruct(values.shape, values.dtype),
        in_specs=[anywhere] * 2,
        out_specs=anywhere,
        input_output_aliases={0: 0},
        compiler_params=pltpu.CompilerParams(vmem_limit_bytes=1024 * 1024),
        name="after",
    )(values, earlier)


def nt(left, right):
    return lax.dot_general(left, right, (((1,), (1,)), ((), ())), preferred_element_type=F32)


def nn(left, right):
    return jnp.dot(left, right, preferred_element_type=F32)


def places(ids, experts, capacity):
    top, rows = ids.shape
    kinds = lax.broadcasted_iota(jnp.int32, (experts, rows), 0)
    named = jnp.zeros((experts, rows), F32)
    for k in range(top):
        named = named + jnp.where(ids[k : k + 1, :] == kinds, 1.0, 0.0)
    earlier = jnp.where(
        lax.broadcasted_iota(jnp.int32, (rows, rows), 0)
        < lax.broadcasted_iota(jnp.int32, (rows, rows), 1),
        1.0,
        0.0,
    )
    before = nn(named.astype(BF16), earlier.astype(BF16))
    place = before + kinds.astype(F32) * capacity
    return [
        jnp.sum(jnp.where(ids[k : k + 1, :] == kinds, place, 0.0), axis=0, keepdims=True)
        for k in range(top)
    ]


def pack_kernel(*refs):
    sources, (sent_ref, joined_ref), targets = refs[:7], refs[7:9], refs[9:16]
    ids_ref, comb_ref, tok_ref, cot_ref = targets[3:]
    held_ref, sems, load_sems = refs[16:]
    loads = [
        pltpu.make_async_copy(source, target, load_sems.at[n])
        for n, (source, target) in enumerate(zip(sources, targets))
    ]
    for load in loads:
        load.start()
    ff = joined_ref.shape[1] // 3
    for m, load in enumerate(loads[:3]):
        load.wait()
        joined_ref[:, m * ff : (m + 1) * ff] = targets[m][0]
    loads = loads[3:]
    top, rows = ids_ref.shape
    experts, capacity = sent_ref.shape[0], sent_ref.shape[1] // 2
    slots = experts * capacity
    slot_iota = lax.broadcasted_iota(jnp.int32, (slots, rows), 0).astype(F32)
    spread = jnp.zeros((slots, rows), F32)
    weight = jnp.zeros((slots, rows), F32)
    loads[0].wait()
    loads[1].wait()
    for k, slot in enumerate(places(ids_ref[...], experts, capacity)):
        hot = jnp.where(slot_iota == slot, 1.0, 0.0)
        spread = spread + hot
        weight = weight + hot * comb_ref[k : k + 1, :]
    spread = spread.astype(BF16)
    loads[2].wait()
    put_rows(held_ref, 0, nn(spread, tok_ref[...]).astype(BF16))
    first = send_out(held_ref, sent_ref, sems, 0)
    loads[3].wait()
    cot_rows = nn(spread, cot_ref[...])
    put_rows(held_ref, 1, (cot_rows * jnp.sum(weight, axis=1, keepdims=True)).astype(BF16))
    second = send_out(held_ref, sent_ref, sems, 1)
    first.wait()
    second.wait()


def put_rows(held_ref, half, values, columns=slice(None)):
    experts, capacity = held_ref.shape[0], held_ref.shape[1] // 2
    for e in range(experts):
        held_ref[e, half * capacity : (half + 1) * capacity, columns] = values[
            e * capacity : (e + 1) * capacity
        ]


def take_rows(ref, half):
    experts, capacity = ref.shape[0], ref.shape[1] // 2
    return jnp.concatenate(
        [ref[e, half * capacity : (half + 1) * capacity] for e in range(experts)], axis=0
    )


def send_out(held_ref, out_ref, sems, half):
    capacity = held_ref.shape[1] // 2
    part = pl.ds(half * capacity, capacity)
    copy = pltpu.make_async_copy(held_ref.at[:, part], out_ref.at[:, part], sems.at[half])
    copy.start()
    return copy


def pick_kernel(experts, capacity, ids_ref, comb_ref, late_ref, pick_ref, ccol_ref):
    del late_ref
    top, rows = ids_ref.shape
    slots = experts * capacity
    slot_iota = lax.broadcasted_iota(jnp.int32, (slots, rows), 0).astype(F32)
    for k, slot in enumerate(places(ids_ref[...], experts, capacity)):
        pick_ref[k] = jnp.transpose(jnp.where(slot_iota == slot, 1.0, 0.0)).astype(BF16)
    padded = jnp.concatenate([comb_ref[...], jnp.zeros((rows - top, rows), F32)], axis=0)
    ccol_ref[...] = jnp.transpose(padded)


def order_kernel(zs, order_ref):
    width = order_ref.shape[0]
    dp = lax.axis_index("dp")
    core = lax.rem(lax.axis_index("expert"), CORES)
    my_z, my_y = dp // NY, lax.rem(dp, NY)
    depth = width // (zs * NY)
    i = lax.broadcasted_iota(jnp.int32, (1, width), 1)
    r = lax.rem(i, depth)
    pos = lax.rem(i // depth, zs // PAR)
    step = i // (depth * zs)
    other = lax.rem(i // (depth * (zs // PAR)), PAR)
    zi = jnp.where(core == 0, pos, zs // PAR - 1 - pos)
    ahead = jnp.where(step == 1, -1, jnp.where(step == 2, 1, step - step // 3))
    y = lax.rem(my_y + NY + jnp.where(core == 0, ahead, -ahead), NY)
    z = zi * PAR + lax.rem(my_z + other, PAR)
    feature = (z * NY + y) * depth + r
    tile = 128

    def one(t, carry):
        d = lax.broadcasted_iota(jnp.int32, (tile, width), 0) + t * tile
        order_ref[pl.ds(pl.multiple_of(t * tile, tile), tile), :] = jnp.where(
            d == feature, 1.0, 0.0
        ).astype(BF16)
        return carry

    lax.fori_loop(0, width // tile, one, 0)


def turn_kernel(rows_ref, order_ref, tok_ref, grad_ref):
    tok_ref[...] = nn(take_rows(rows_ref, 0), order_ref[...]).astype(BF16)
    grad_ref[...] = nn(take_rows(rows_ref, 1), order_ref[...]).astype(BF16)


def pair(pieces, columns):
    return jnp.concatenate([piece[:, columns] for piece in pieces], axis=0)


def partial_kernel(tok_ref, grad_ref, *refs):
    pieces, sums = refs[:-3], refs[-3:]
    ff = sums[0].shape[1]
    tile, depth = 256, 2 * pieces[0].shape[0]
    for m, (out_ref, rows_ref) in enumerate(zip(sums, (tok_ref, tok_ref, grad_ref))):
        for t in range(ff // tile):
            columns = slice(m * ff + t * tile, m * ff + (t + 1) * tile)
            total = None
            for j in range(len(pieces) // 2):
                part = nn(
                    rows_ref[:, j * depth : (j + 1) * depth],
                    pair(pieces[2 * j : 2 * j + 2], columns),
                )
                total = part if total is None else total + part
            out_ref[:, t * tile : (t + 1) * tile] = total


def final_kernel(count, tok_ref, grad_ref, order_ref, *refs):
    sums, pieces = refs[:3], refs[3 : 3 + count]
    out_ref, late_ref, hidden_ref, gate_grad_ref, up_grad_ref, arr_ref, held_ref, sems = refs[3 + count :]
    late_ref[...] = jnp.zeros_like(late_ref)
    ff, width = hidden_ref.shape[1], order_ref.shape[0]
    tile, depth = 256, 2 * pieces[0].shape[0]
    last = slice(width - depth, width)
    for t in range(ff // tile):
        here = slice(t * tile, (t + 1) * tile)
        gate, up, hidden_grad = (
            sums[m][:, here]
            + nn(rows_ref[:, last], pair(pieces[-2:], slice(m * ff + t * tile, m * ff + (t + 1) * tile)))
            for m, rows_ref in enumerate((tok_ref, tok_ref, grad_ref))
        )
        sigma = 1.0 / (1.0 + jnp.exp(-gate))
        silu = gate * sigma
        hidden_ref[:, here] = (silu * up).astype(BF16)
        up_grad_ref[:, here] = (hidden_grad * silu).astype(BF16)
        gate_grad_ref[:, here] = (hidden_grad * up * sigma * (1.0 + gate * (1.0 - sigma))).astype(BF16)
    copies = []
    for half, terms in enumerate((((hidden_ref, 2),), ((gate_grad_ref, 0), (up_grad_ref, 1)))):
        for j in range(count // 2):
            total = None
            for left_ref, m in terms:
                part = nt(left_ref[...], pair(pieces[2 * j : 2 * j + 2], slice(m * ff, (m + 1) * ff)))
                total = part if total is None else total + part
            arr_ref[half, :, j * depth : (j + 1) * depth] = total.astype(BF16)
        for t in range(width // tile):
            here = slice(t * tile, (t + 1) * tile)
            put_rows(held_ref, half, nt(arr_ref[half], order_ref[here, :]).astype(BF16), here)
        copies.append(send_out(held_ref, out_ref, sems, half))
    for copy in copies:
        copy.wait()


def post_kernel(pick_ref, ccol_ref, cot_ref, back_ref, mixed_ref, igrad_ref, cgrad_ref):
    top, rows, _ = pick_ref.shape
    cot = cot_ref[...].astype(F32)
    back = take_rows(back_ref, 0)
    lane = lax.broadcasted_iota(jnp.int32, (rows, rows), 1)
    mixed = jnp.zeros(cot.shape, F32)
    grads = jnp.zeros((rows, rows), F32)
    both = None
    for k in range(top):
        out = nn(pick_ref[k], back)
        mixed = mixed + ccol_ref[:, k : k + 1] * out
        grads = jnp.where(lane == k, jnp.sum(cot * out, axis=1, keepdims=True), grads)
        both = pick_ref[k] if both is None else both + pick_ref[k]
    mixed_ref[...] = mixed.astype(BF16)
    cgrad_ref[...] = jnp.transpose(grads)[:top, :]
    igrad_ref[...] = nn(both, take_rows(back_ref, 1)).astype(BF16)


def on_device(tokens, expert_ids, combine, w_gate, w_up, w_down, cotangent):
    groups = lax.axis_size("expert")
    zs = lax.axis_size("dp") // NY
    rows, top = expert_ids.shape
    width = tokens.shape[1]
    ff = w_gate.shape[2]
    capacity = 3 * rows * top // (2 * groups)
    slots = groups * capacity
    shape = jax.ShapeDtypeStruct

    def device(z, y, e):
        return ((z % zs) * NY + y % NY) * groups + e

    def shifted(dz, dy):
        return [
            (device(z, y, e), device(z + s * dz, y + s * dy, e))
            for z in range(zs)
            for y in range(NY)
            for e in range(groups)
            for s in ((1, -1)[e % CORES],)
        ]

    far_groups = [
        [device(z, y, e) for z in range(par, zs, PAR)][:: (1, -1)[e % CORES]]
        for par in range(PAR)
        for y in range(NY)
        for e in range(groups)
    ]

    def swap(values):
        return lax.all_to_all(values, "expert", 0, 0, tiled=True)

    def send(values, dz, dy):
        return lax.ppermute(values, ALL, shifted(dz, dy))

    spec = pl.BlockSpec(memory_space=pltpu.VMEM)
    both = shape((groups, 2 * capacity, width), BF16)
    ids, weights = expert_ids.T, combine.T
    depth = w_gate.shape[1]
    hbm = pl.BlockSpec(memory_space=pltpu.HBM)
    sources = (w_gate, w_up, w_down, ids, weights, tokens, cotangent)
    sent, joined = pl.pallas_call(
        pack_kernel,
        out_shape=(both, shape((depth, 3 * ff), BF16)),
        in_specs=[hbm] * len(sources),
        out_specs=(hbm, spec),
        scratch_shapes=[pltpu.VMEM(v.shape, v.dtype) for v in sources]
        + [
            pltpu.VMEM(both.shape, BF16),
            pltpu.SemaphoreType.DMA((2,)),
            pltpu.SemaphoreType.DMA((len(sources),)),
        ],
        compiler_params=pltpu.CompilerParams(vmem_limit_bytes=12 * 1024 * 1024),
        name="pack",
    )(*(pltpu.with_memory_space_constraint(v, pltpu.HBM) for v in sources))
    arrived = swap(sent)
    own = lax.all_gather(joined, ALL, axis=0, tiled=True, axis_index_groups=far_groups)
    own = after(own, arrived)
    ahead, beside, behind = send(own, 0, 1), send(own, 1, 0), send(own, 0, -1)
    across = send(ahead, 0, 1)
    pieces = [own, beside, ahead, send(beside, 0, 1), behind, send(behind, 1, 0)]
    pieces += [across, send(across, 1, 0)]
    count = len(pieces)
    order = call(lambda ref: order_kernel(zs, ref), "order", shape((width, width), BF16))
    rows_shape, sum_shape = shape((slots, width), BF16), shape((slots, ff), F32)
    turned = call(turn_kernel, "turn", (rows_shape,) * 2, arrived, order)
    sums = call(partial_kernel, "partial", (sum_shape,) * 3, *turned, *pieces[:-2], mib=12)
    results, late = pl.pallas_call(
        lambda *refs: final_kernel(count, *refs),
        out_shape=(pltpu.HBM(both.shape, BF16), shape((8, 128), F32)),
        in_specs=[spec] * (6 + count),
        out_specs=(hbm, spec),
        scratch_shapes=[pltpu.VMEM((slots, ff), BF16)] * 3
        + [
            pltpu.VMEM((2, slots, width), BF16),
            pltpu.VMEM(both.shape, BF16),
            pltpu.SemaphoreType.DMA((2,)),
        ],
        compiler_params=pltpu.CompilerParams(vmem_limit_bytes=20 * 1024 * 1024),
        name="final",
    )(*turned, order, *sums, *pieces)
    back = swap(results)
    pick, ccol = pl.pallas_call(
        lambda *refs: pick_kernel(groups, capacity, *refs),
        out_shape=(shape((top, rows, slots), BF16), shape((rows, rows), F32)),
        in_specs=[spec] * 3,
        out_specs=(spec,) * 2,
        compiler_params=pltpu.CompilerParams(vmem_limit_bytes=8 * 1024 * 1024),
        name="pick",
    )(ids, weights, late)
    mixed, input_grad, combine_grad = call(
        post_kernel,
        "post",
        (shape((rows, width), BF16),) * 2 + (shape((top, rows), F32),),
        pick,
        ccol,
        cotangent,
        back,
    )
    return mixed, input_grad, combine_grad.T


def solution(mesh):
    rows = P(ALL, None)
    weights = P("expert", "dp", None)
    return jax.shard_map(
        on_device,
        mesh=mesh,
        in_specs=(rows, rows, rows, weights, weights, weights, rows),
        out_specs=(rows, rows, rows),
        check_vma=False,
    )
```

```python
import jax
import jax.numpy as jnp
from jax import lax
from jax.experimental import pallas as pl
from jax.experimental.pallas import tpu as pltpu
from jax.sharding import PartitionSpec as P

F32 = jnp.float32
BF16 = jnp.bfloat16
ALL = ("dp", "expert")
NY, CORES, PAR = 4, 2, 2


def call(body, name, out_shape, *args, mib=16):
    spec = pl.BlockSpec(memory_space=pltpu.VMEM)
    many = isinstance(out_shape, tuple)
    return pl.pallas_call(
        body,
        out_shape=out_shape,
        in_specs=[spec] * len(args),
        out_specs=(spec,) * len(out_shape) if many else spec,
        compiler_params=pltpu.CompilerParams(vmem_limit_bytes=mib * 1024 * 1024),
        name=name,
    )(*args)


def after(values, earlier):
    anywhere = pl.BlockSpec(memory_space=pl.ANY)
    return pl.pallas_call(
        lambda *refs: None,
        out_shape=jax.ShapeDtypeStruct(values.shape, values.dtype),
        in_specs=[anywhere] * 2,
        out_specs=anywhere,
        input_output_aliases={0: 0},
        compiler_params=pltpu.CompilerParams(vmem_limit_bytes=1024 * 1024),
        name="after",
    )(values, earlier)


def nt(left, right):
    return lax.dot_general(left, right, (((1,), (1,)), ((), ())), preferred_element_type=F32)


def nn(left, right):
    return jnp.dot(left, right, preferred_element_type=F32)


def places(ids, experts, capacity):
    top, rows = ids.shape
    kinds = lax.broadcasted_iota(jnp.int32, (experts, rows), 0)
    named = jnp.zeros((experts, rows), F32)
    for k in range(top):
        named = named + jnp.where(ids[k : k + 1, :] == kinds, 1.0, 0.0)
    earlier = jnp.where(
        lax.broadcasted_iota(jnp.int32, (rows, rows), 0)
        < lax.broadcasted_iota(jnp.int32, (rows, rows), 1),
        1.0,
        0.0,
    )
    before = nn(named.astype(BF16), earlier.astype(BF16))
    place = before + kinds.astype(F32) * capacity
    return [
        jnp.sum(jnp.where(ids[k : k + 1, :] == kinds, place, 0.0), axis=0, keepdims=True)
        for k in range(top)
    ]


def pack_kernel(*refs):
    sources, (sent_ref, joined_ref), targets = refs[:7], refs[7:9], refs[9:16]
    ids_ref, comb_ref, tok_ref, cot_ref = targets[3:]
    held_ref, sems, load_sems = refs[16:]
    loads = [
        pltpu.make_async_copy(source, target, load_sems.at[n])
        for n, (source, target) in enumerate(zip(sources, targets))
    ]
    for load in loads:
        load.start()
    ff = joined_ref.shape[1] // 3
    for m, load in enumerate(loads[:3]):
        load.wait()
        joined_ref[:, m * ff : (m + 1) * ff] = targets[m][0]
    loads = loads[3:]
    top, rows = ids_ref.shape
    experts, capacity = sent_ref.shape[0], sent_ref.shape[1] // 2
    slots = experts * capacity
    slot_iota = lax.broadcasted_iota(jnp.int32, (slots, rows), 0).astype(F32)
    spread = jnp.zeros((slots, rows), F32)
    weight = jnp.zeros((slots, rows), F32)
    loads[0].wait()
    loads[1].wait()
    for k, slot in enumerate(places(ids_ref[...], experts, capacity)):
        hot = jnp.where(slot_iota == slot, 1.0, 0.0)
        spread = spread + hot
        weight = weight + hot * comb_ref[k : k + 1, :]
    spread = spread.astype(BF16)
    loads[2].wait()
    put_rows(held_ref, 0, nn(spread, tok_ref[...]).astype(BF16))
    first = send_out(held_ref, sent_ref, sems, 0)
    loads[3].wait()
    cot_rows = nn(spread, cot_ref[...])
    put_rows(held_ref, 1, (cot_rows * jnp.sum(weight, axis=1, keepdims=True)).astype(BF16))
    second = send_out(held_ref, sent_ref, sems, 1)
    first.wait()
    second.wait()


def put_rows(held_ref, half, values, columns=slice(None)):
    experts, capacity = held_ref.shape[0], held_ref.shape[1] // 2
    for e in range(experts):
        held_ref[e, half * capacity : (half + 1) * capacity, columns] = values[
            e * capacity : (e + 1) * capacity
        ]


def take_rows(ref, half):
    experts, capacity = ref.shape[0], ref.shape[1] // 2
    return jnp.concatenate(
        [ref[e, half * capacity : (half + 1) * capacity] for e in range(experts)], axis=0
    )


def send_out(held_ref, out_ref, sems, half):
    capacity = held_ref.shape[1] // 2
    part = pl.ds(half * capacity, capacity)
    copy = pltpu.make_async_copy(held_ref.at[:, part], out_ref.at[:, part], sems.at[half])
    copy.start()
    return copy


def pick_kernel(experts, capacity, ids_ref, comb_ref, late_ref, pick_ref, ccol_ref):
    del late_ref
    top, rows = ids_ref.shape
    slots = experts * capacity
    slot_iota = lax.broadcasted_iota(jnp.int32, (slots, rows), 0).astype(F32)
    for k, slot in enumerate(places(ids_ref[...], experts, capacity)):
        pick_ref[k] = jnp.transpose(jnp.where(slot_iota == slot, 1.0, 0.0)).astype(BF16)
    padded = jnp.concatenate([comb_ref[...], jnp.zeros((rows - top, rows), F32)], axis=0)
    ccol_ref[...] = jnp.transpose(padded)


def order_kernel(zs, order_ref):
    width = order_ref.shape[0]
    dp = lax.axis_index("dp")
    core = lax.rem(lax.axis_index("expert"), CORES)
    my_z, my_y = dp // NY, lax.rem(dp, NY)
    depth = width // (zs * NY)
    i = lax.broadcasted_iota(jnp.int32, (1, width), 1)
    r = lax.rem(i, depth)
    pos = lax.rem(i // depth, zs // PAR)
    step = i // (depth * zs)
    other = lax.rem(i // (depth * (zs // PAR)), PAR)
    zi = jnp.where(core == 0, pos, zs // PAR - 1 - pos)
    ahead = jnp.where(step == 1, -1, jnp.where(step == 2, 2, step // 3))
    y = lax.rem(my_y + NY + jnp.where(core == 0, ahead, -ahead), NY)
    z = zi * PAR + lax.rem(my_z + other, PAR)
    feature = (z * NY + y) * depth + r
    tile = 128

    def one(t, carry):
        d = lax.broadcasted_iota(jnp.int32, (tile, width), 0) + t * tile
        order_ref[pl.ds(pl.multiple_of(t * tile, tile), tile), :] = jnp.where(
            d == feature, 1.0, 0.0
        ).astype(BF16)
        return carry

    lax.fori_loop(0, width // tile, one, 0)


def turn_kernel(rows_ref, order_ref, tok_ref, grad_ref):
    tok_ref[...] = nn(take_rows(rows_ref, 0), order_ref[...]).astype(BF16)
    grad_ref[...] = nn(take_rows(rows_ref, 1), order_ref[...]).astype(BF16)


def pair(pieces, columns):
    return jnp.concatenate([piece[:, columns] for piece in pieces], axis=0)


def partial_kernel(tok_ref, grad_ref, *refs):
    pieces, sums = refs[:-3], refs[-3:]
    ff = sums[0].shape[1]
    tile, depth = 256, 2 * pieces[0].shape[0]
    for m, (out_ref, rows_ref) in enumerate(zip(sums, (tok_ref, tok_ref, grad_ref))):
        for t in range(ff // tile):
            columns = slice(m * ff + t * tile, m * ff + (t + 1) * tile)
            total = None
            for j in range(len(pieces) // 2):
                part = nn(
                    rows_ref[:, j * depth : (j + 1) * depth],
                    pair(pieces[2 * j : 2 * j + 2], columns),
                )
                total = part if total is None else total + part
            out_ref[:, t * tile : (t + 1) * tile] = total


def final_kernel(count, tok_ref, grad_ref, order_ref, *refs):
    sums, pieces = refs[:3], refs[3 : 3 + count]
    out_ref, late_ref, hidden_ref, gate_grad_ref, up_grad_ref, arr_ref, held_ref, sems = refs[3 + count :]
    late_ref[...] = jnp.zeros_like(late_ref)
    ff, width = hidden_ref.shape[1], order_ref.shape[0]
    tile, depth = 256, 2 * pieces[0].shape[0]
    last = slice(width - depth, width)
    for t in range(ff // tile):
        here = slice(t * tile, (t + 1) * tile)
        gate, up, hidden_grad = (
            sums[m][:, here]
            + nn(rows_ref[:, last], pair(pieces[-2:], slice(m * ff + t * tile, m * ff + (t + 1) * tile)))
            for m, rows_ref in enumerate((tok_ref, tok_ref, grad_ref))
        )
        sigma = 1.0 / (1.0 + jnp.exp(-gate))
        silu = gate * sigma
        hidden_ref[:, here] = (silu * up).astype(BF16)
        up_grad_ref[:, here] = (hidden_grad * silu).astype(BF16)
        gate_grad_ref[:, here] = (hidden_grad * up * sigma * (1.0 + gate * (1.0 - sigma))).astype(BF16)
    copies = []
    for half, terms in enumerate((((hidden_ref, 2),), ((gate_grad_ref, 0), (up_grad_ref, 1)))):
        for j in range(count // 2):
            total = None
            for left_ref, m in terms:
                part = nt(left_ref[...], pair(pieces[2 * j : 2 * j + 2], slice(m * ff, (m + 1) * ff)))
                total = part if total is None else total + part
            arr_ref[half, :, j * depth : (j + 1) * depth] = total.astype(BF16)
        for t in range(width // tile):
            here = slice(t * tile, (t + 1) * tile)
            put_rows(held_ref, half, nt(arr_ref[half], order_ref[here, :]).astype(BF16), here)
        copies.append(send_out(held_ref, out_ref, sems, half))
    for copy in copies:
        copy.wait()


def post_kernel(pick_ref, ccol_ref, cot_ref, back_ref, mixed_ref, igrad_ref, cgrad_ref):
    top, rows, _ = pick_ref.shape
    cot = cot_ref[...].astype(F32)
    back = take_rows(back_ref, 0)
    lane = lax.broadcasted_iota(jnp.int32, (rows, rows), 1)
    mixed = jnp.zeros(cot.shape, F32)
    grads = jnp.zeros((rows, rows), F32)
    both = None
    for k in range(top):
        out = nn(pick_ref[k], back)
        mixed = mixed + ccol_ref[:, k : k + 1] * out
        grads = jnp.where(lane == k, jnp.sum(cot * out, axis=1, keepdims=True), grads)
        both = pick_ref[k] if both is None else both + pick_ref[k]
    mixed_ref[...] = mixed.astype(BF16)
    cgrad_ref[...] = jnp.transpose(grads)[:top, :]
    igrad_ref[...] = nn(both, take_rows(back_ref, 1)).astype(BF16)


def on_device(tokens, expert_ids, combine, w_gate, w_up, w_down, cotangent):
    groups = lax.axis_size("expert")
    zs = lax.axis_size("dp") // NY
    rows, top = expert_ids.shape
    width = tokens.shape[1]
    ff = w_gate.shape[2]
    capacity = 3 * rows * top // (2 * groups)
    slots = groups * capacity
    shape = jax.ShapeDtypeStruct

    def device(z, y, e):
        return ((z % zs) * NY + y % NY) * groups + e

    def shifted(dz, dy):
        return [
            (device(z, y, e), device(z + s * dz, y + s * dy, e))
            for z in range(zs)
            for y in range(NY)
            for e in range(groups)
            for s in ((1, -1)[e % CORES],)
        ]

    far_groups = [
        [device(z, y, e) for z in range(par, zs, PAR)][:: (1, -1)[e % CORES]]
        for par in range(PAR)
        for y in range(NY)
        for e in range(groups)
    ]

    def swap(values):
        return lax.all_to_all(values, "expert", 0, 0, tiled=True)

    def send(values, dz, dy):
        return lax.ppermute(values, ALL, shifted(dz, dy))

    spec = pl.BlockSpec(memory_space=pltpu.VMEM)
    both = shape((groups, 2 * capacity, width), BF16)
    ids, weights = expert_ids.T, combine.T
    depth = w_gate.shape[1]
    hbm = pl.BlockSpec(memory_space=pltpu.HBM)
    sources = (w_gate, w_up, w_down, ids, weights, tokens, cotangent)
    sent, joined = pl.pallas_call(
        pack_kernel,
        out_shape=(both, shape((depth, 3 * ff), BF16)),
        in_specs=[hbm] * len(sources),
        out_specs=(hbm, spec),
        scratch_shapes=[pltpu.VMEM(v.shape, v.dtype) for v in sources]
        + [
            pltpu.VMEM(both.shape, BF16),
            pltpu.SemaphoreType.DMA((2,)),
            pltpu.SemaphoreType.DMA((len(sources),)),
        ],
        compiler_params=pltpu.CompilerParams(vmem_limit_bytes=12 * 1024 * 1024),
        name="pack",
    )(*(pltpu.with_memory_space_constraint(v, pltpu.HBM) for v in sources))
    arrived = swap(sent)
    own = lax.all_gather(joined, ALL, axis=0, tiled=True, axis_index_groups=far_groups)
    own = after(own, arrived)
    ahead, beside, behind = send(own, 0, 1), send(own, 1, 0), send(own, 0, -1)
    pieces = [own, beside, ahead, send(ahead, 1, 0), send(ahead, 0, 1), send(ahead, 1, 1)]
    pieces += [behind, send(behind, 1, 0)]
    count = len(pieces)
    order = call(lambda ref: order_kernel(zs, ref), "order", shape((width, width), BF16))
    rows_shape, sum_shape = shape((slots, width), BF16), shape((slots, ff), F32)
    turned = call(turn_kernel, "turn", (rows_shape,) * 2, arrived, order)
    sums = call(partial_kernel, "partial", (sum_shape,) * 3, *turned, *pieces[:-2], mib=12)
    results, late = pl.pallas_call(
        lambda *refs: final_kernel(count, *refs),
        out_shape=(pltpu.HBM(both.shape, BF16), shape((8, 128), F32)),
        in_specs=[spec] * (6 + count),
        out_specs=(hbm, spec),
        scratch_shapes=[pltpu.VMEM((slots, ff), BF16)] * 3
        + [
            pltpu.VMEM((2, slots, width), BF16),
            pltpu.VMEM(both.shape, BF16),
            pltpu.SemaphoreType.DMA((2,)),
        ],
        compiler_params=pltpu.CompilerParams(vmem_limit_bytes=20 * 1024 * 1024),
        name="final",
    )(*turned, order, *sums, *pieces)
    back = swap(results)
    pick, ccol = pl.pallas_call(
        lambda *refs: pick_kernel(groups, capacity, *refs),
        out_shape=(shape((top, rows, slots), BF16), shape((rows, rows), F32)),
        in_specs=[spec] * 3,
        out_specs=(spec,) * 2,
        compiler_params=pltpu.CompilerParams(vmem_limit_bytes=8 * 1024 * 1024),
        name="pick",
    )(ids, weights, late)
    mixed, input_grad, combine_grad = call(
        post_kernel,
        "post",
        (shape((rows, width), BF16),) * 2 + (shape((top, rows), F32),),
        pick,
        ccol,
        cotangent,
        back,
    )
    return mixed, input_grad, combine_grad.T


def solution(mesh):
    rows = P(ALL, None)
    weights = P("expert", "dp", None)
    return jax.shard_map(
        on_device,
        mesh=mesh,
        in_specs=(rows, rows, rows, weights, weights, weights, rows),
        out_specs=(rows, rows, rows),
        check_vma=False,
    )
```

```python
import jax
import jax.numpy as jnp
from jax import lax
from jax.experimental import pallas as pl
from jax.experimental.pallas import tpu as pltpu
from jax.sharding import PartitionSpec as P

F32 = jnp.float32
BF16 = jnp.bfloat16
ALL = ("dp", "expert")
NY, CORES, PAR = 4, 2, 2


def call(body, name, out_shape, *args, mib=16):
    spec = pl.BlockSpec(memory_space=pltpu.VMEM)
    many = isinstance(out_shape, tuple)
    return pl.pallas_call(
        body,
        out_shape=out_shape,
        in_specs=[spec] * len(args),
        out_specs=(spec,) * len(out_shape) if many else spec,
        compiler_params=pltpu.CompilerParams(vmem_limit_bytes=mib * 1024 * 1024),
        name=name,
    )(*args)


def after(values, earlier):
    anywhere = pl.BlockSpec(memory_space=pl.ANY)
    return pl.pallas_call(
        lambda *refs: None,
        out_shape=jax.ShapeDtypeStruct(values.shape, values.dtype),
        in_specs=[anywhere] * 2,
        out_specs=anywhere,
        input_output_aliases={0: 0},
        compiler_params=pltpu.CompilerParams(vmem_limit_bytes=1024 * 1024),
        name="after",
    )(values, earlier)


def nt(left, right):
    return lax.dot_general(left, right, (((1,), (1,)), ((), ())), preferred_element_type=F32)


def nn(left, right):
    return jnp.dot(left, right, preferred_element_type=F32)


def places(ids, experts, capacity):
    top, rows = ids.shape
    kinds = lax.broadcasted_iota(jnp.int32, (experts, rows), 0)
    named = jnp.zeros((experts, rows), F32)
    for k in range(top):
        named = named + jnp.where(ids[k : k + 1, :] == kinds, 1.0, 0.0)
    earlier = jnp.where(
        lax.broadcasted_iota(jnp.int32, (rows, rows), 0)
        < lax.broadcasted_iota(jnp.int32, (rows, rows), 1),
        1.0,
        0.0,
    )
    before = nn(named.astype(BF16), earlier.astype(BF16))
    place = before + kinds.astype(F32) * capacity
    return [
        jnp.sum(jnp.where(ids[k : k + 1, :] == kinds, place, 0.0), axis=0, keepdims=True)
        for k in range(top)
    ]


def pack_kernel(*refs):
    sources, (sent_ref, joined_ref), targets = refs[:7], refs[7:9], refs[9:16]
    ids_ref, comb_ref, tok_ref, cot_ref = targets[3:]
    held_ref, sems, load_sems = refs[16:]
    loads = [
        pltpu.make_async_copy(source, target, load_sems.at[n])
        for n, (source, target) in enumerate(zip(sources, targets))
    ]
    for load in loads:
        load.start()
    ff = joined_ref.shape[1] // 3
    for m, load in enumerate(loads[:3]):
        load.wait()
        joined_ref[:, m * ff : (m + 1) * ff] = targets[m][0]
    loads = loads[3:]
    top, rows = ids_ref.shape
    experts, capacity = sent_ref.shape[0], sent_ref.shape[1] // 2
    slots = experts * capacity
    slot_iota = lax.broadcasted_iota(jnp.int32, (slots, rows), 0).astype(F32)
    spread = jnp.zeros((slots, rows), F32)
    weight = jnp.zeros((slots, rows), F32)
    loads[0].wait()
    loads[1].wait()
    for k, slot in enumerate(places(ids_ref[...], experts, capacity)):
        hot = jnp.where(slot_iota == slot, 1.0, 0.0)
        spread = spread + hot
        weight = weight + hot * comb_ref[k : k + 1, :]
    spread = spread.astype(BF16)
    loads[2].wait()
    put_rows(held_ref, 0, nn(spread, tok_ref[...]).astype(BF16))
    first = send_out(held_ref, sent_ref, sems, 0)
    loads[3].wait()
    cot_rows = nn(spread, cot_ref[...])
    put_rows(held_ref, 1, (cot_rows * jnp.sum(weight, axis=1, keepdims=True)).astype(BF16))
    second = send_out(held_ref, sent_ref, sems, 1)
    first.wait()
    second.wait()


def put_rows(held_ref, half, values, columns=slice(None)):
    experts, capacity = held_ref.shape[0], held_ref.shape[1] // 2
    for e in range(experts):
        held_ref[e, half * capacity : (half + 1) * capacity, columns] = values[
            e * capacity : (e + 1) * capacity
        ]


def take_rows(ref, half):
    experts, capacity = ref.shape[0], ref.shape[1] // 2
    return jnp.concatenate(
        [ref[e, half * capacity : (half + 1) * capacity] for e in range(experts)], axis=0
    )


def send_out(held_ref, out_ref, sems, half):
    capacity = held_ref.shape[1] // 2
    part = pl.ds(half * capacity, capacity)
    copy = pltpu.make_async_copy(held_ref.at[:, part], out_ref.at[:, part], sems.at[half])
    copy.start()
    return copy


def pick_kernel(experts, capacity, ids_ref, comb_ref, late_ref, pick_ref, ccol_ref):
    del late_ref
    top, rows = ids_ref.shape
    slots = experts * capacity
    slot_iota = lax.broadcasted_iota(jnp.int32, (slots, rows), 0).astype(F32)
    for k, slot in enumerate(places(ids_ref[...], experts, capacity)):
        pick_ref[k] = jnp.transpose(jnp.where(slot_iota == slot, 1.0, 0.0)).astype(BF16)
    padded = jnp.concatenate([comb_ref[...], jnp.zeros((rows - top, rows), F32)], axis=0)
    ccol_ref[...] = jnp.transpose(padded)


def order_kernel(zs, order_ref):
    width = order_ref.shape[0]
    dp = lax.axis_index("dp")
    core = lax.rem(lax.axis_index("expert"), CORES)
    my_z, my_y = dp // NY, lax.rem(dp, NY)
    depth = width // (zs * NY)
    i = lax.broadcasted_iota(jnp.int32, (1, width), 1)
    r = lax.rem(i, depth)
    pos = lax.rem(i // depth, zs // PAR)
    step = i // (depth * zs)
    other = lax.rem(i // (depth * (zs // PAR)), PAR)
    zi = jnp.where(core == 0, pos, zs // PAR - 1 - pos)
    ahead = jnp.where(step == 1, -1, jnp.where(step == 2, 1, step - step // 3))
    y = lax.rem(my_y + NY + jnp.where(core == 0, ahead, -ahead), NY)
    z = zi * PAR + lax.rem(my_z + other, PAR)
    feature = (z * NY + y) * depth + r
    tile = 128

    def one(t, carry):
        d = lax.broadcasted_iota(jnp.int32, (tile, width), 0) + t * tile
        order_ref[pl.ds(pl.multiple_of(t * tile, tile), tile), :] = jnp.where(
            d == feature, 1.0, 0.0
        ).astype(BF16)
        return carry

    lax.fori_loop(0, width // tile, one, 0)


def turn_kernel(rows_ref, order_ref, tok_ref, grad_ref):
    tok_ref[...] = nn(take_rows(rows_ref, 0), order_ref[...]).astype(BF16)
    grad_ref[...] = nn(take_rows(rows_ref, 1), order_ref[...]).astype(BF16)


def pair(pieces, columns):
    return jnp.concatenate([piece[:, columns] for piece in pieces], axis=0)


def partial_kernel(tok_ref, grad_ref, *refs):
    pieces, sums = refs[:-3], refs[-3:]
    ff = sums[0].shape[1]
    tile, depth = 256, 2 * pieces[0].shape[0]
    for m, (out_ref, rows_ref) in enumerate(zip(sums, (tok_ref, tok_ref, grad_ref))):
        for t in range(ff // tile):
            columns = slice(m * ff + t * tile, m * ff + (t + 1) * tile)
            total = None
            for j in range(len(pieces) // 2):
                part = nn(
                    rows_ref[:, j * depth : (j + 1) * depth],
                    pair(pieces[2 * j : 2 * j + 2], columns),
                )
                total = part if total is None else total + part
            out_ref[:, t * tile : (t + 1) * tile] = total


def final_kernel(count, tok_ref, grad_ref, order_ref, *refs):
    sums, pieces = refs[:3], refs[3 : 3 + count]
    out_ref, late_ref, hidden_ref, gate_grad_ref, up_grad_ref, arr_ref, held_ref, sems = refs[3 + count :]
    late_ref[...] = jnp.zeros_like(late_ref)
    ff, width = hidden_ref.shape[1], order_ref.shape[0]
    tile, depth = 256, 2 * pieces[0].shape[0]
    last = slice(width - depth, width)
    for t in range(ff // tile):
        here = slice(t * tile, (t + 1) * tile)
        gate, up, hidden_grad = (
            sums[m][:, here]
            + nn(rows_ref[:, last], pair(pieces[-2:], slice(m * ff + t * tile, m * ff + (t + 1) * tile)))
            for m, rows_ref in enumerate((tok_ref, tok_ref, grad_ref))
        )
        sigma = 1.0 / (1.0 + jnp.exp(-gate))
        silu = gate * sigma
        hidden_ref[:, here] = (silu * up).astype(BF16)
        up_grad_ref[:, here] = (hidden_grad * silu).astype(BF16)
        gate_grad_ref[:, here] = (hidden_grad * up * sigma * (1.0 + gate * (1.0 - sigma))).astype(BF16)
    copies = []
    for half, terms in enumerate((((hidden_ref, 2),), ((gate_grad_ref, 0), (up_grad_ref, 1)))):
        for j in range(count // 2):
            total = None
            for left_ref, m in terms:
                part = nt(left_ref[...], pair(pieces[2 * j : 2 * j + 2], slice(m * ff, (m + 1) * ff)))
                total = part if total is None else total + part
            arr_ref[half, :, j * depth : (j + 1) * depth] = total.astype(BF16)
        for t in range(width // tile):
            here = slice(t * tile, (t + 1) * tile)
            put_rows(held_ref, half, nt(arr_ref[half], order_ref[here, :]).astype(BF16), here)
        copies.append(send_out(held_ref, out_ref, sems, half))
    for copy in copies:
        copy.wait()


def post_kernel(pick_ref, ccol_ref, cot_ref, back_ref, mixed_ref, igrad_ref, cgrad_ref):
    top, rows, _ = pick_ref.shape
    cot = cot_ref[...].astype(F32)
    back = take_rows(back_ref, 0)
    lane = lax.broadcasted_iota(jnp.int32, (rows, rows), 1)
    mixed = jnp.zeros(cot.shape, F32)
    grads = jnp.zeros((rows, rows), F32)
    both = None
    for k in range(top):
        out = nn(pick_ref[k], back)
        mixed = mixed + ccol_ref[:, k : k + 1] * out
        grads = jnp.where(lane == k, jnp.sum(cot * out, axis=1, keepdims=True), grads)
        both = pick_ref[k] if both is None else both + pick_ref[k]
    mixed_ref[...] = mixed.astype(BF16)
    cgrad_ref[...] = jnp.transpose(grads)[:top, :]
    igrad_ref[...] = nn(both, take_rows(back_ref, 1)).astype(BF16)


def on_device(tokens, expert_ids, combine, w_gate, w_up, w_down, cotangent):
    groups = lax.axis_size("expert")
    zs = lax.axis_size("dp") // NY
    rows, top = expert_ids.shape
    width = tokens.shape[1]
    ff = w_gate.shape[2]
    capacity = 3 * rows * top // (2 * groups)
    slots = groups * capacity
    shape = jax.ShapeDtypeStruct

    def device(z, y, e):
        return ((z % zs) * NY + y % NY) * groups + e

    def shifted(dz, dy):
        return [
            (device(z, y, e), device(z + s * dz, y + s * dy, e))
            for z in range(zs)
            for y in range(NY)
            for e in range(groups)
            for s in ((1, -1)[e % CORES],)
        ]

    far_groups = [
        [device(z, y, e) for z in range(par, zs, PAR)][:: (1, -1)[e % CORES]]
        for par in range(PAR)
        for y in range(NY)
        for e in range(groups)
    ]

    def swap(values):
        return lax.all_to_all(values, "expert", 0, 0, tiled=True)

    def send(values, dz, dy):
        return lax.ppermute(values, ALL, shifted(dz, dy))

    spec = pl.BlockSpec(memory_space=pltpu.VMEM)
    both = shape((groups, 2 * capacity, width), BF16)
    ids, weights = expert_ids.T, combine.T
    depth = w_gate.shape[1]
    hbm = pl.BlockSpec(memory_space=pltpu.HBM)
    sources = (w_gate, w_up, w_down, ids, weights, tokens, cotangent)
    sent, joined = pl.pallas_call(
        pack_kernel,
        out_shape=(both, shape((depth, 3 * ff), BF16)),
        in_specs=[hbm] * len(sources),
        out_specs=(hbm, spec),
        scratch_shapes=[pltpu.VMEM(v.shape, v.dtype) for v in sources]
        + [
            pltpu.VMEM(both.shape, BF16),
            pltpu.SemaphoreType.DMA((2,)),
            pltpu.SemaphoreType.DMA((len(sources),)),
        ],
        compiler_params=pltpu.CompilerParams(vmem_limit_bytes=12 * 1024 * 1024),
        name="pack",
    )(*(pltpu.with_memory_space_constraint(v, pltpu.HBM) for v in sources))
    arrived = swap(sent)
    own = lax.all_gather(joined, ALL, axis=0, tiled=True, axis_index_groups=far_groups)
    own = after(own, arrived)
    ahead, beside, behind = send(own, 0, 1), send(own, 1, 0), send(own, 0, -1)
    pieces = [own, beside, ahead, send(ahead, 1, 0), behind, send(own, 1, -1)]
    pieces += [send(ahead, 0, 1), send(ahead, 1, 1)]
    count = len(pieces)
    order = call(lambda ref: order_kernel(zs, ref), "order", shape((width, width), BF16))
    rows_shape, sum_shape = shape((slots, width), BF16), shape((slots, ff), F32)
    turned = call(turn_kernel, "turn", (rows_shape,) * 2, arrived, order)
    sums = call(partial_kernel, "partial", (sum_shape,) * 3, *turned, *pieces[:-2], mib=12)
    results, late = pl.pallas_call(
        lambda *refs: final_kernel(count, *refs),
        out_shape=(pltpu.HBM(both.shape, BF16), shape((8, 128), F32)),
        in_specs=[spec] * (6 + count),
        out_specs=(hbm, spec),
        scratch_shapes=[pltpu.VMEM((slots, ff), BF16)] * 3
        + [
            pltpu.VMEM((2, slots, width), BF16),
            pltpu.VMEM(both.shape, BF16),
            pltpu.SemaphoreType.DMA((2,)),
        ],
        compiler_params=pltpu.CompilerParams(vmem_limit_bytes=20 * 1024 * 1024),
        name="final",
    )(*turned, order, *sums, *pieces)
    back = swap(results)
    pick, ccol = pl.pallas_call(
        lambda *refs: pick_kernel(groups, capacity, *refs),
        out_shape=(shape((top, rows, slots), BF16), shape((rows, rows), F32)),
        in_specs=[spec] * 3,
        out_specs=(spec,) * 2,
        compiler_params=pltpu.CompilerParams(vmem_limit_bytes=8 * 1024 * 1024),
        name="pick",
    )(ids, weights, late)
    mixed, input_grad, combine_grad = call(
        post_kernel,
        "post",
        (shape((rows, width), BF16),) * 2 + (shape((top, rows), F32),),
        pick,
        ccol,
        cotangent,
        back,
    )
    return mixed, input_grad, combine_grad.T


def solution(mesh):
    rows = P(ALL, None)
    weights = P("expert", "dp", None)
    return jax.shard_map(
        on_device,
        mesh=mesh,
        in_specs=(rows, rows, rows, weights, weights, weights, rows),
        out_specs=(rows, rows, rows),
        check_vma=False,
    )
```

```python
import jax
import jax.numpy as jnp
from jax import lax
from jax.experimental import pallas as pl
from jax.experimental.pallas import tpu as pltpu
from jax.sharding import PartitionSpec as P

F32 = jnp.float32
BF16 = jnp.bfloat16
ALL = ("dp", "expert")
NY, CORES, PAR = 4, 2, 2


def call(body, name, out_shape, *args, mib=16):
    spec = pl.BlockSpec(memory_space=pltpu.VMEM)
    many = isinstance(out_shape, tuple)
    return pl.pallas_call(
        body,
        out_shape=out_shape,
        in_specs=[spec] * len(args),
        out_specs=(spec,) * len(out_shape) if many else spec,
        compiler_params=pltpu.CompilerParams(vmem_limit_bytes=mib * 1024 * 1024),
        name=name,
    )(*args)


def after(values, earlier):
    anywhere = pl.BlockSpec(memory_space=pl.ANY)
    return pl.pallas_call(
        lambda *refs: None,
        out_shape=jax.ShapeDtypeStruct(values.shape, values.dtype),
        in_specs=[anywhere] * 2,
        out_specs=anywhere,
        input_output_aliases={0: 0},
        compiler_params=pltpu.CompilerParams(vmem_limit_bytes=1024 * 1024),
        name="after",
    )(values, earlier)


def nt(left, right):
    return lax.dot_general(left, right, (((1,), (1,)), ((), ())), preferred_element_type=F32)


def nn(left, right):
    return jnp.dot(left, right, preferred_element_type=F32)


def places(ids, experts, capacity):
    top, rows = ids.shape
    kinds = lax.broadcasted_iota(jnp.int32, (experts, rows), 0)
    named = jnp.zeros((experts, rows), F32)
    for k in range(top):
        named = named + jnp.where(ids[k : k + 1, :] == kinds, 1.0, 0.0)
    earlier = jnp.where(
        lax.broadcasted_iota(jnp.int32, (rows, rows), 0)
        < lax.broadcasted_iota(jnp.int32, (rows, rows), 1),
        1.0,
        0.0,
    )
    before = nn(named.astype(BF16), earlier.astype(BF16))
    place = before + kinds.astype(F32) * capacity
    return [
        jnp.sum(jnp.where(ids[k : k + 1, :] == kinds, place, 0.0), axis=0, keepdims=True)
        for k in range(top)
    ]


def pack_kernel(*refs):
    sources, (sent_ref, joined_ref), targets = refs[:7], refs[7:9], refs[9:16]
    ids_ref, comb_ref, tok_ref, cot_ref = targets[3:]
    held_ref, sems, load_sems = refs[16:]
    loads = [
        pltpu.make_async_copy(source, target, load_sems.at[n])
        for n, (source, target) in enumerate(zip(sources, targets))
    ]
    for load in loads:
        load.start()
    ff = joined_ref.shape[1] // 3
    for m, load in enumerate(loads[:3]):
        load.wait()
        joined_ref[:, m * ff : (m + 1) * ff] = targets[m][0]
    loads = loads[3:]
    top, rows = ids_ref.shape
    experts, capacity = sent_ref.shape[0], sent_ref.shape[1] // 2
    slots = experts * capacity
    slot_iota = lax.broadcasted_iota(jnp.int32, (slots, rows), 0).astype(F32)
    spread = jnp.zeros((slots, rows), F32)
    weight = jnp.zeros((slots, rows), F32)
    loads[0].wait()
    loads[1].wait()
    for k, slot in enumerate(places(ids_ref[...], experts, capacity)):
        hot = jnp.where(slot_iota == slot, 1.0, 0.0)
        spread = spread + hot
        weight = weight + hot * comb_ref[k : k + 1, :]
    spread = spread.astype(BF16)
    loads[2].wait()
    put_rows(held_ref, 0, nn(spread, tok_ref[...]).astype(BF16))
    first = send_out(held_ref, sent_ref, sems, 0)
    loads[3].wait()
    cot_rows = nn(spread, cot_ref[...])
    put_rows(held_ref, 1, (cot_rows * jnp.sum(weight, axis=1, keepdims=True)).astype(BF16))
    second = send_out(held_ref, sent_ref, sems, 1)
    first.wait()
    second.wait()


def put_rows(held_ref, half, values, columns=slice(None)):
    experts, capacity = held_ref.shape[0], held_ref.shape[1] // 2
    for e in range(experts):
        held_ref[e, half * capacity : (half + 1) * capacity, columns] = values[
            e * capacity : (e + 1) * capacity
        ]


def take_rows(ref, half):
    experts, capacity = ref.shape[0], ref.shape[1] // 2
    return jnp.concatenate(
        [ref[e, half * capacity : (half + 1) * capacity] for e in range(experts)], axis=0
    )


def send_out(held_ref, out_ref, sems, half):
    capacity = held_ref.shape[1] // 2
    part = pl.ds(half * capacity, capacity)
    copy = pltpu.make_async_copy(held_ref.at[:, part], out_ref.at[:, part], sems.at[half])
    copy.start()
    return copy


def pick_kernel(experts, capacity, ids_ref, comb_ref, late_ref, pick_ref, ccol_ref):
    del late_ref
    top, rows = ids_ref.shape
    slots = experts * capacity
    slot_iota = lax.broadcasted_iota(jnp.int32, (slots, rows), 0).astype(F32)
    for k, slot in enumerate(places(ids_ref[...], experts, capacity)):
        pick_ref[k] = jnp.transpose(jnp.where(slot_iota == slot, 1.0, 0.0)).astype(BF16)
    padded = jnp.concatenate([comb_ref[...], jnp.zeros((rows - top, rows), F32)], axis=0)
    ccol_ref[...] = jnp.transpose(padded)


def order_kernel(zs, order_ref):
    width = order_ref.shape[0]
    dp = lax.axis_index("dp")
    core = lax.rem(lax.axis_index("expert"), CORES)
    my_z, my_y = dp // NY, lax.rem(dp, NY)
    depth = width // (zs * NY)
    i = lax.broadcasted_iota(jnp.int32, (1, width), 1)
    r = lax.rem(i, depth)
    pos = lax.rem(i // depth, zs // PAR)
    block = i // (depth * (zs // PAR))
    other = jnp.where(block < 4, lax.rem(block, 2), block // 6)
    zi = jnp.where(core == 0, pos, zs // PAR - 1 - pos)
    ahead = jnp.where(block < 2, 0, jnp.where(block < 4, 2, 2 * lax.rem(block, 2) - 1))
    y = lax.rem(my_y + NY + jnp.where(core == 0, ahead, -ahead), NY)
    z = zi * PAR + lax.rem(my_z + other, PAR)
    feature = (z * NY + y) * depth + r
    tile = 128

    def one(t, carry):
        d = lax.broadcasted_iota(jnp.int32, (tile, width), 0) + t * tile
        order_ref[pl.ds(pl.multiple_of(t * tile, tile), tile), :] = jnp.where(
            d == feature, 1.0, 0.0
        ).astype(BF16)
        return carry

    lax.fori_loop(0, width // tile, one, 0)


def turn_kernel(rows_ref, order_ref, tok_ref, grad_ref):
    tok_ref[...] = nn(take_rows(rows_ref, 0), order_ref[...]).astype(BF16)
    grad_ref[...] = nn(take_rows(rows_ref, 1), order_ref[...]).astype(BF16)


def pair(pieces, columns):
    return jnp.concatenate([piece[:, columns] for piece in pieces], axis=0)


def partial_kernel(tok_ref, grad_ref, *refs):
    pieces, sums = refs[:-3], refs[-3:]
    ff = sums[0].shape[1]
    tile, depth = 256, 2 * pieces[0].shape[0]
    for m, (out_ref, rows_ref) in enumerate(zip(sums, (tok_ref, tok_ref, grad_ref))):
        for t in range(ff // tile):
            columns = slice(m * ff + t * tile, m * ff + (t + 1) * tile)
            total = None
            for j in range(len(pieces) // 2):
                part = nn(
                    rows_ref[:, j * depth : (j + 1) * depth],
                    pair(pieces[2 * j : 2 * j + 2], columns),
                )
                total = part if total is None else total + part
            out_ref[:, t * tile : (t + 1) * tile] = total


def final_kernel(count, tok_ref, grad_ref, order_ref, *refs):
    sums, pieces = refs[:3], refs[3 : 3 + count]
    out_ref, late_ref, hidden_ref, gate_grad_ref, up_grad_ref, arr_ref, held_ref, sems = refs[3 + count :]
    late_ref[...] = jnp.zeros_like(late_ref)
    ff, width = hidden_ref.shape[1], order_ref.shape[0]
    tile, depth = 256, 2 * pieces[0].shape[0]
    last = slice(width - depth, width)
    for t in range(ff // tile):
        here = slice(t * tile, (t + 1) * tile)
        gate, up, hidden_grad = (
            sums[m][:, here]
            + nn(rows_ref[:, last], pair(pieces[-1:], slice(m * ff + t * tile, m * ff + (t + 1) * tile)))
            for m, rows_ref in enumerate((tok_ref, tok_ref, grad_ref))
        )
        sigma = 1.0 / (1.0 + jnp.exp(-gate))
        silu = gate * sigma
        hidden_ref[:, here] = (silu * up).astype(BF16)
        up_grad_ref[:, here] = (hidden_grad * silu).astype(BF16)
        gate_grad_ref[:, here] = (hidden_grad * up * sigma * (1.0 + gate * (1.0 - sigma))).astype(BF16)
    copies = []
    for half, terms in enumerate((((hidden_ref, 2),), ((gate_grad_ref, 0), (up_grad_ref, 1)))):
        for j in range((count + 1) // 2):
            total = None
            for left_ref, m in terms:
                part = nt(left_ref[...], pair(pieces[2 * j : 2 * j + 2], slice(m * ff, (m + 1) * ff)))
                total = part if total is None else total + part
            arr_ref[half, :, j * depth : (j + 1) * depth] = total.astype(BF16)
        for t in range(width // tile):
            here = slice(t * tile, (t + 1) * tile)
            put_rows(held_ref, half, nt(arr_ref[half], order_ref[here, :]).astype(BF16), here)
        copies.append(send_out(held_ref, out_ref, sems, half))
    for copy in copies:
        copy.wait()


def post_kernel(pick_ref, ccol_ref, cot_ref, back_ref, mixed_ref, igrad_ref, cgrad_ref):
    top, rows, _ = pick_ref.shape
    cot = cot_ref[...].astype(F32)
    back = take_rows(back_ref, 0)
    lane = lax.broadcasted_iota(jnp.int32, (rows, rows), 1)
    mixed = jnp.zeros(cot.shape, F32)
    grads = jnp.zeros((rows, rows), F32)
    both = None
    for k in range(top):
        out = nn(pick_ref[k], back)
        mixed = mixed + ccol_ref[:, k : k + 1] * out
        grads = jnp.where(lane == k, jnp.sum(cot * out, axis=1, keepdims=True), grads)
        both = pick_ref[k] if both is None else both + pick_ref[k]
    mixed_ref[...] = mixed.astype(BF16)
    cgrad_ref[...] = jnp.transpose(grads)[:top, :]
    igrad_ref[...] = nn(both, take_rows(back_ref, 1)).astype(BF16)


def on_device(tokens, expert_ids, combine, w_gate, w_up, w_down, cotangent):
    groups = lax.axis_size("expert")
    zs = lax.axis_size("dp") // NY
    rows, top = expert_ids.shape
    width = tokens.shape[1]
    ff = w_gate.shape[2]
    capacity = 3 * rows * top // (2 * groups)
    slots = groups * capacity
    shape = jax.ShapeDtypeStruct

    def device(z, y, e):
        return ((z % zs) * NY + y % NY) * groups + e

    def shifted(dz, dy):
        return [
            (device(z, y, e), device(z + s * dz, y + s * dy, e))
            for z in range(zs)
            for y in range(NY)
            for e in range(groups)
            for s in ((1, -1)[e % CORES],)
        ]

    far_groups = [
        [device(z, y, e) for z in range(par, zs, PAR)][:: (1, -1)[e % CORES]]
        for par in range(PAR)
        for y in range(NY)
        for e in range(groups)
    ]

    def swap(values):
        return lax.all_to_all(values, "expert", 0, 0, tiled=True)

    def send(values, dz, dy):
        return lax.ppermute(values, ALL, shifted(dz, dy))

    spec = pl.BlockSpec(memory_space=pltpu.VMEM)
    both = shape((groups, 2 * capacity, width), BF16)
    ids, weights = expert_ids.T, combine.T
    depth = w_gate.shape[1]
    hbm = pl.BlockSpec(memory_space=pltpu.HBM)
    sources = (w_gate, w_up, w_down, ids, weights, tokens, cotangent)
    sent, joined = pl.pallas_call(
        pack_kernel,
        out_shape=(both, shape((depth, 3 * ff), BF16)),
        in_specs=[hbm] * len(sources),
        out_specs=(hbm, spec),
        scratch_shapes=[pltpu.VMEM(v.shape, v.dtype) for v in sources]
        + [
            pltpu.VMEM(both.shape, BF16),
            pltpu.SemaphoreType.DMA((2,)),
            pltpu.SemaphoreType.DMA((len(sources),)),
        ],
        compiler_params=pltpu.CompilerParams(vmem_limit_bytes=12 * 1024 * 1024),
        name="pack",
    )(*(pltpu.with_memory_space_constraint(v, pltpu.HBM) for v in sources))
    arrived = swap(sent)
    own = lax.all_gather(joined, ALL, axis=0, tiled=True, axis_index_groups=far_groups)
    own = after(own, arrived)
    ahead, beside, behind = send(own, 0, 1), send(own, 1, 0), send(own, 0, -1)
    pieces = [own, beside, send(ahead, 0, 1), send(ahead, 1, 1), ahead, behind]
    pieces.append(send(after(jnp.concatenate([ahead, behind], axis=0), beside), 1, 0))
    count = len(pieces)
    order = call(lambda ref: order_kernel(zs, ref), "order", shape((width, width), BF16))
    rows_shape, sum_shape = shape((slots, width), BF16), shape((slots, ff), F32)
    turned = call(turn_kernel, "turn", (rows_shape,) * 2, arrived, order)
    sums = call(partial_kernel, "partial", (sum_shape,) * 3, *turned, *pieces[:-1], mib=12)
    results, late = pl.pallas_call(
        lambda *refs: final_kernel(count, *refs),
        out_shape=(pltpu.HBM(both.shape, BF16), shape((8, 128), F32)),
        in_specs=[spec] * (6 + count),
        out_specs=(hbm, spec),
        scratch_shapes=[pltpu.VMEM((slots, ff), BF16)] * 3
        + [
            pltpu.VMEM((2, slots, width), BF16),
            pltpu.VMEM(both.shape, BF16),
            pltpu.SemaphoreType.DMA((2,)),
        ],
        compiler_params=pltpu.CompilerParams(vmem_limit_bytes=20 * 1024 * 1024),
        name="final",
    )(*turned, order, *sums, *pieces)
    back = swap(results)
    pick, ccol = pl.pallas_call(
        lambda *refs: pick_kernel(groups, capacity, *refs),
        out_shape=(shape((top, rows, slots), BF16), shape((rows, rows), F32)),
        in_specs=[spec] * 3,
        out_specs=(spec,) * 2,
        compiler_params=pltpu.CompilerParams(vmem_limit_bytes=8 * 1024 * 1024),
        name="pick",
    )(ids, weights, late)
    mixed, input_grad, combine_grad = call(
        post_kernel,
        "post",
        (shape((rows, width), BF16),) * 2 + (shape((top, rows), F32),),
        pick,
        ccol,
        cotangent,
        back,
    )
    return mixed, input_grad, combine_grad.T


def solution(mesh):
    rows = P(ALL, None)
    weights = P("expert", "dp", None)
    return jax.shard_map(
        on_device,
        mesh=mesh,
        in_specs=(rows, rows, rows, weights, weights, weights, rows),
        out_specs=(rows, rows, rows),
        check_vma=False,
    )
```
